128 devices in a mesh: row: 8 (over x_lo, y), col: 16 (over x_hi, z, core).
Axes of the slice: x: 4 (x_hi: 2, x_lo: 2; x = x_hi * 2 + x_lo), y: 4, z: 4, core: 2. Of those that a mesh axis runs over, the one named last changes fastest.
Arguments:
- rhs: bfloat16 [1024, 2, 4096], P('col', None, 'row'), may hold values from -6 to 6
- solved: bfloat16 [1024, 49152], P(None, 'col'), may hold values from -6 to 6
- panel: bfloat16 [2, 4096, 49152], P(None, 'row', 'col'), may hold values from -0.02734375 to 0.02734375
- inverse: bfloat16 [2, 4096, 4096], P(None, 'row'), as said below
- link: bfloat16 [4096, 4096], P('row'), may hold values from -0.09375 to 0.09375
Outputs:
- solution: bfloat16 [1024, 2, 4096], P('col', None, 'row')
The draws below stay inside these ranges and needn't reach their ends.
Inputs may be any that keep to these rules, and one draw needn't show every extreme that they name: Each inverse[b] is upper triangular with diagonal entries between 0.6 and 1.4.
All inputs are finite; a program needn't handle non-finite values.
Results may differ from the reference program's by a relative error of at most 0.0056.
Values may be sent and summed in bfloat16 or wider, within the bound.
A program may use at most 128 MiB of HBM per device.

```python
import jax
import jax.numpy as jnp

BLOCK = 4096
SAMPLES = 1024
PRIOR = 49152


def draw_inverse(key, part):
    key_off = jax.random.fold_in(key, 11)
    key_diag = jax.random.fold_in(key, 12)
    values = jax.random.normal(key_off, (2, BLOCK, BLOCK), jnp.float32)
    rows_idx = jnp.arange(BLOCK)[:, None]
    cols_idx = jnp.arange(BLOCK)[None, :]
    upper = (rows_idx < cols_idx).astype(jnp.float32)
    same = (rows_idx == cols_idx).astype(jnp.float32)
    diag_vals = jax.random.uniform(key_diag, (2, 1, BLOCK), jnp.float32, 0.6, 1.4)
    scale = 0.8 / jnp.sqrt(jnp.float32(BLOCK))
    return (values * upper[None] * scale + same[None] * diag_vals).astype(jnp.bfloat16)


def strengthened(result, rng, source, target, blocks, factor):
    owner, partner = [(jnp.arange(result.shape[axis_at]) // (result.shape[axis_at] // blocks)).reshape([-1 if axis == axis_at else 1 for axis in range(result.ndim)]) for axis_at in (source, target)]
    chosen = jax.random.permutation(rng, blocks)[partner]
    strong = (owner == chosen) | (owner == (partner + blocks // 2) % blocks)
    return jnp.where(strong, factor * result, result)


def steps_of(rng, dims, shards, low, largest):
    gain = 1.0
    for axis_at, blocks in shards:
        heights = jax.random.uniform(jax.random.fold_in(jax.random.fold_in(rng, 6), axis_at), (blocks,), jnp.float32, low / len(shards), largest / len(shards))
        gain = gain * jnp.repeat(jnp.exp(heights), dims[axis_at] // blocks).reshape((-1,) + (1,) * (len(dims) - 1 - axis_at))
    return gain


def gaussian(stream_key, dims, scale, reach, pieces=(), kind=jnp.bfloat16):
    result = jax.random.normal(stream_key, dims, jnp.float32) * scale
    if len(pieces) > 0:
        result = steps_of(stream_key, dims, pieces, -0.22, 0.18) * result
    return jnp.clip(result, min=-reach, max=reach).astype(kind)


def gaussian_with(rng, shape, spread, most, split, heavy, dtype=jnp.bfloat16):
    values = spread * jax.random.normal(rng, shape, jnp.float32)
    if split:
        values = values * steps_of(rng, shape, split, -0.22, 0.18)
    return jnp.clip(strengthened(values, jax.random.fold_in(rng, 3), *heavy), -most, most).astype(dtype)


def setup_inputs(seed: int = 0) -> dict:
    key_list = jax.random.split(jax.random.key(seed), 6)
    rhs = gaussian(key_list[0], (SAMPLES, 2, BLOCK), 1.0, 6.0, ((0, 16), (2, 8)))
    solved = gaussian_with(key_list[1], (SAMPLES, PRIOR), 1.0, 6.0, ((1, 16),), (1, 0, 16, 2.0))
    panel = gaussian(key_list[2], (2, BLOCK, PRIOR), PRIOR ** -0.5, 0.02734375, ((1, 8), (2, 16)))
    inverse = draw_inverse(jax.random.fold_in(key_list[5], 71), 0)
    link = gaussian(key_list[4], (BLOCK, BLOCK), BLOCK ** -0.5, 0.09375, ((0, 8),))
    return dict(rhs=rhs, solved=solved, panel=panel, inverse=inverse, link=link)


def reference(rhs, solved, panel, inverse, link):
    flat_panel = panel.reshape(2 * BLOCK, PRIOR)
    sums = jnp.dot(solved, flat_panel.T, preferred_element_type=jnp.float32).reshape(SAMPLES, 2, BLOCK)
    first_res = (rhs[:, 0, :].astype(jnp.float32) - sums[:, 0, :]).astype(jnp.bfloat16)
    first = jnp.dot(first_res, inverse[0], preferred_element_type=jnp.float32).astype(jnp.bfloat16)
    carried = jnp.dot(first, link.T, preferred_element_type=jnp.float32)
    second_res = (rhs[:, 1, :].astype(jnp.float32) - sums[:, 1, :] - carried).astype(jnp.bfloat16)
    second = jnp.dot(second_res, inverse[1], preferred_element_type=jnp.float32).astype(jnp.bfloat16)
    return jnp.stack([first, second], axis=1)
```

```python
import functools

import jax
import jax.numpy as jnp
from jax import lax
from jax.experimental import pallas as pl
from jax.experimental.pallas import tpu as pltpu
from jax.sharding import PartitionSpec as P

MESH = pl.DeviceIdType.MESH
BF16 = jnp.bfloat16
F32 = jnp.float32
NT = (((1,), (1,)), ((), ()))
NN = (((1,), (0,)), ((), ()))
ROWS = 8
Z_OFFSETS = (2, 1, 3, 0)


def dot(left, right, dims):
    return lax.dot_general(left, right, dims, preferred_element_type=F32)


def kernel(
    solved, panel, inverse, link, rhs, out,
    sol_v, pan_v, inv_v, lnk_v, rhs_v,
    core_out, core_in, own, col_out, col_in, res1,
    a_out, a_in, f_all, c_out, c_in,
    load_sem, core_sem, col_sem, a_sem, f_sem, c_sem,
):
    samples, local_rows = rhs.shape[1], rhs.shape[2]
    row, col = lax.axis_index("row"), lax.axis_index("col")
    x_hi, z, core = col // 8, (col // 2) % 4, col % 2

    def col_of(dx, dz, k):
        return lax.rem(x_hi + dx, 2) * 8 + lax.rem(z + dz, 4) * 2 + k

    def rows(slot, count=1):
        return pl.ds(slot * samples, count * samples)

    def remote(src, dst, sems, slot, device):
        return pltpu.make_async_remote_copy(
            src_ref=src, dst_ref=dst, send_sem=sems.at[0, slot], recv_sem=sems.at[1, slot],
            device_id=device, device_id_type=MESH,
        )

    def load_sol(kind, half, j):
        c = col_of(1 - half, Z_OFFSETS[j], 1 - core if kind == 0 else core)
        slot = kind * 8 + half * 4 + j
        return pltpu.make_async_copy(
            solved.at[pl.ds(pl.multiple_of(c * samples, samples), samples)],
            sol_v.at[rows(slot)], load_sem.at[slot],
        )

    load_panel = [pltpu.make_async_copy(panel.at[b], pan_v.at[b], load_sem.at[16 + b]) for b in range(2)]
    load_inv = [pltpu.make_async_copy(inverse.at[b], inv_v.at[b], load_sem.at[18 + b]) for b in range(2)]
    load_link = pltpu.make_async_copy(link, lnk_v, load_sem.at[20])
    load_rhs = pltpu.make_async_copy(rhs, rhs_v, load_sem.at[21])
    load_panel[0].start()
    for half in range(2):
        for kind in range(2):
            for j in range(4):
                load_sol(kind, half, j).start()
    load_panel[1].start()
    load_rhs.start()
    load_inv[0].start()
    load_link.start()
    load_inv[1].start()

    barrier = pltpu.get_barrier_semaphore()
    for i in range(1, ROWS):
        pl.semaphore_signal(barrier, inc=1, device_id=(lax.rem(row + i, ROWS), col), device_id_type=MESH)
    for dx in range(2):
        for dz in range(4):
            if dx or dz:
                pl.semaphore_signal(barrier, inc=1, device_id=(row, col_of(dx, dz, core)), device_id_type=MESH)
    sibling = (row, col_of(0, 0, 1 - core))
    pl.semaphore_signal(barrier, inc=1, device_id=sibling, device_id_type=MESH)
    pl.semaphore_wait(barrier, 15)

    def core_copy(b, half):
        at = rows(half * 4, 4)
        return remote(core_out.at[b, at], core_in.at[b, at], core_sem, b * 2 + half, sibling)

    def col_copy(b, half, j):
        at = rows(half * 4 + j)
        return remote(
            col_out.at[b, at], col_in.at[b, at], col_sem, b * 8 + half * 4 + j,
            (row, col_of(1 - half, Z_OFFSETS[j], core)),
        )

    for b in range(2):
        load_panel[b].wait()
        for half in range(2):
            at = rows(half * 4, 4)
            if b == 0:
                for j in range(4):
                    load_sol(0, half, j).wait()
            core_out[b, at] = dot(sol_v[at], pan_v[b], NT).astype(BF16)
            core_copy(b, half).start()
            if b == 0:
                for j in range(4):
                    load_sol(1, half, j).wait()
            own[...] = dot(sol_v[rows(8 + half * 4, 4)], pan_v[b], NT)
            core_copy(b, half).wait_recv()
            total = own[...] + core_in[b, at].astype(F32)
            if half == 0:
                col_out[b, at] = total.astype(BF16)
            else:
                col_out[b, rows(4, 3)] = total[: 3 * samples].astype(BF16)
                res1[b] = total[3 * samples :]
            for j in range(4):
                if half == 0 or j < 3:
                    col_copy(b, half, j).start()

    def summed(b):
        total = res1[b]
        for half in range(2):
            for j in range(4):
                if half == 0 or j < 3:
                    col_copy(b, half, j).wait_recv()
                    total = total + col_in[b, rows(half * 4 + j)].astype(F32)
        return total

    def cols(index):
        return pl.ds(pl.multiple_of(index * local_rows, local_rows), local_rows)

    def solve(b, res, outgoing, incoming, sems, wait_between=None):
        def copy(i):
            return remote(outgoing.at[i], incoming.at[i], sems, i, (row + i, col))

        for i in reversed(range(1, ROWS)):
            @pl.when(row + i < ROWS)
            def _():
                outgoing[i] = dot(res, inv_v[b, :, cols(row + i)], NN).astype(BF16)
                copy(i).start()

        res1[b] = dot(res, inv_v[b, :, cols(row)], NN)
        for i in range(1, ROWS):
            @pl.when(row >= i)
            def _():
                copy(i).wait_recv()
                res1[b] += incoming[i].astype(F32)

        for i in range(1, ROWS):
            @pl.when(row + i < ROWS)
            def _():
                copy(i).wait_send()

        return res1[b].astype(BF16)

    load_rhs.wait()
    res0 = (rhs_v[0].astype(F32) - summed(0)).astype(BF16)
    load_inv[0].wait()
    first = solve(0, res0, a_out, a_in, a_sem)
    f_all[0] = first
    out[0] = first

    def f_copy(i):
        return remote(f_all.at[0], f_all.at[i], f_sem, i, (lax.rem(row + i, ROWS), col))

    for i in range(1, ROWS):
        f_copy(i).start()
    rest = rhs_v[1].astype(F32) - summed(1)
    load_link.wait()
    rest = rest - dot(f_all[0], lnk_v[:, cols(row)], NT)
    res1[1] = rest
    for i in range(1, ROWS):
        f_copy(i).wait_recv()
        res1[1] -= dot(f_all[i], lnk_v[:, cols(lax.rem(row + ROWS - i, ROWS))], NT)
    load_inv[1].wait()
    out[1] = solve(1, res1[1].astype(BF16), c_out, c_in, c_sem)

    for i in range(1, ROWS):
        f_copy(i).wait_send()
    for b in range(2):
        for half in range(2):
            core_copy(b, half).wait_send()
            for j in range(4):
                if half == 0 or j < 3:
                    col_copy(b, half, j).wait_send()


def local(rhs, solved, panel, inverse, link):
    samples, _, local_rows = rhs.shape
    depth, total = solved.shape[1], solved.shape[0]
    block = (samples, local_rows)
    any_spec = pl.BlockSpec(memory_space=pl.ANY)
    parts = pl.pallas_call(
        kernel,
        out_shape=jax.ShapeDtypeStruct((2,) + block, BF16),
        in_specs=[any_spec] * 5,
        out_specs=pl.BlockSpec(memory_space=pltpu.VMEM),
        scratch_shapes=[
            pltpu.VMEM(solved.shape, BF16),
            pltpu.VMEM(panel.shape, BF16),
            pltpu.VMEM(inverse.shape, BF16),
            pltpu.VMEM(link.shape, BF16),
            pltpu.VMEM((2,) + block, BF16),
            pltpu.VMEM((2, 8 * samples, local_rows), BF16),
            pltpu.VMEM((2, 8 * samples, local_rows), BF16),
            pltpu.VMEM((4 * samples, local_rows), F32),
            pltpu.VMEM((2, 8 * samples, local_rows), BF16),
            pltpu.VMEM((2, 8 * samples, local_rows), BF16),
            pltpu.VMEM((2,) + block, F32),
            pltpu.VMEM((8,) + block, BF16),
            pltpu.VMEM((8,) + block, BF16),
            pltpu.VMEM((8,) + block, BF16),
            pltpu.VMEM((8,) + block, BF16),
            pltpu.VMEM((8,) + block, BF16),
            pltpu.SemaphoreType.DMA((22,)),
            pltpu.SemaphoreType.DMA((2, 4)),
            pltpu.SemaphoreType.DMA((2, 16)),
            pltpu.SemaphoreType.DMA((2, 8)),
            pltpu.SemaphoreType.DMA((2, 8)),
            pltpu.SemaphoreType.DMA((2, 8)),
        ],
        compiler_params=pltpu.CompilerParams(
            collective_id=0, has_side_effects=True, vmem_limit_bytes=56 << 20
        ),
        cost_estimate=pl.CostEstimate(
            flops=4 * total * depth * local_rows, bytes_accessed=24 << 20, transcendentals=0
        ),
        name="window_solve",
    )(solved, panel, inverse, link, rhs.transpose(1, 0, 2))
    return parts.transpose(1, 0, 2)


def solution(mesh):
    return jax.shard_map(
        local,
        mesh=mesh,
        in_specs=(
            P("col", None, "row"),
            P(None, "col"),
            P(None, "row", "col"),
            P(None, "row", None),
            P("row", None),
        ),
        out_specs=P("col", None, "row"),
        check_vma=False,
    )
```

```python
import functools

import jax
import jax.numpy as jnp
from jax import lax
from jax.experimental import pallas as pl
from jax.experimental.pallas import tpu as pltpu
from jax.sharding import PartitionSpec as P

MESH = pl.DeviceIdType.MESH
BF16 = jnp.bfloat16
F32 = jnp.float32
NT = (((1,), (1,)), ((), ()))
NN = (((1,), (0,)), ((), ()))
ROWS = 8
SLOTS = 8
Z_OFFSETS = (2, 1, 3, 0)
HALVES = 2


def dot(left, right, dims):
    return lax.dot_general(left, right, dims, preferred_element_type=F32)


def kernel(
    stages, solved, panel, inverse, link, rhs, out,
    sol_v, pan_v, inv_v, lnk_v, rhs_v,
    core_out, core_in, col_out, col_in, x_out, x_in, keep, acc,
    part, a_out, a_in, f_all, c_out, c_in,
    load_sem, core_sem, col_sem, x_sem, a_sem, f_sem, c_sem,
):
    samples, local_rows = rhs.shape[0], rhs.shape[2]
    part_rows = samples // HALVES
    row, col = lax.axis_index("row"), lax.axis_index("col")
    x_lo = row // 4
    x_hi, z, core = col // 8, (col // 2) % 4, col % 2
    drains, arrivals = [], {}

    def col_of(dx, dz, k):
        return lax.rem(x_hi + dx, 2) * 8 + lax.rem(z + dz, 4) * 2 + k

    def remote(src, dst, send_sem, recv_sem, device):
        return pltpu.make_async_remote_copy(
            src_ref=src, dst_ref=dst, send_sem=send_sem, recv_sem=recv_sem,
            device_id=device, device_id_type=MESH,
        )

    def start(copy, *key):
        copy.start()
        drains.append(copy.wait_send)
        arrivals[key] = copy.wait_recv

    def arrive(*key):
        arrivals.pop(key)()

    def slot_of(s):
        return Z_OFFSETS[s // 2], 1 - s % 2

    def slot_rows(s, count=1):
        return pl.ds(s * part_rows, count * part_rows)

    def load_sol(kind, h, s):
        dz, dx = slot_of(s)
        c = col_of(dx, dz, 1 - core if kind == 0 else core)
        at = pl.multiple_of(c * samples + h * part_rows, part_rows)
        return pltpu.make_async_copy(
            solved.at[pl.ds(at, part_rows)], sol_v.at[kind, h, slot_rows(s)],
            load_sem.at[(kind * HALVES + h) * SLOTS + s],
        )

    load_panel = [pltpu.make_async_copy(panel.at[b], pan_v.at[b], load_sem.at[32 + b]) for b in range(2)]
    load_inv = [pltpu.make_async_copy(inverse.at[b], inv_v.at[b], load_sem.at[34 + b]) for b in range(2)]
    load_link = pltpu.make_async_copy(link, lnk_v, load_sem.at[36])
    load_rhs = pltpu.make_async_copy(rhs, rhs_v, load_sem.at[37])
    def load(copy, *key):
        copy.start()
        arrivals[key] = copy.wait

    load(load_rhs, "rhs")
    load(load_panel[0], "panel", 0)
    for h in range(HALVES):
        for kind in range(2):
            for s in range(SLOTS):
                load(load_sol(kind, h, s), "sol", kind, h, s)
    load(load_panel[1], "panel", 1)
    load(load_inv[0], "inverse", 0)
    load(load_link, "link")
    load(load_inv[1], "inverse", 1)

    barrier = pltpu.get_barrier_semaphore()
    for i in range(1, ROWS):
        pl.semaphore_signal(barrier, inc=1, device_id=(lax.rem(row + i, ROWS), col), device_id_type=MESH)
    for s in range(SLOTS - 1):
        dz, dx = slot_of(s)
        pl.semaphore_signal(barrier, inc=1, device_id=(row, col_of(dx, dz, core)), device_id_type=MESH)
    sibling = (row, col_of(0, 0, 1 - core))
    pl.semaphore_signal(barrier, inc=1, device_id=sibling, device_id_type=MESH)

    arrive("rhs")
    rhs_all = rhs_v[...].astype(F32)
    for b in range(2):
        for h in range(HALVES):
            acc[b, h] = rhs_all[h * part_rows : (h + 1) * part_rows, b, :]

    pl.semaphore_wait(barrier, 15)

    def core_copy(b, h):
        return remote(core_out.at[b, h], core_in.at[b, h], core_sem.at[0, b, h], core_sem.at[1, b, h], sibling)

    def col_copy(h, s):
        dz, dx = slot_of(s)
        return remote(
            col_out.at[0, h, slot_rows(s)], col_in.at[0, h, slot_rows(s)],
            col_sem.at[0, 0, h, s], col_sem.at[1, 0, h, s], (row, col_of(dx, dz, core)),
        )

    def z_copy(h, i):
        at = slot_rows(2 * i, 2)
        return remote(
            col_out.at[1, h, at], col_in.at[1, h, at],
            col_sem.at[0, 1, h, i], col_sem.at[1, 1, h, i], (row, col_of(0, Z_OFFSETS[i], core)),
        )

    def x_copy(h):
        return remote(x_out.at[h], x_in.at[h], x_sem.at[0, h], x_sem.at[1, h], (row, col_of(1, 0, core)))

    def sibling_part(b, h):
        if b == 0:
            for s in range(SLOTS):
                arrive("sol", 0, h, s)
        if h == 0:
            arrive("panel", b)
        core_out[b, h] = dot(sol_v[0, h], pan_v[b], NT).astype(BF16)
        start(core_copy(b, h), "core", b, h)

    def own_part(b, h):
        if b == 0:
            for s in range(SLOTS):
                arrive("sol", 1, h, s)
        total = dot(sol_v[1, h], pan_v[b], NT)
        arrive("core", b, h)
        total = total + core_in[b, h].astype(F32)
        last = 7 * part_rows
        if b == 0:
            col_out[0, h, slot_rows(0, 7)] = total[:last].astype(BF16)
            for s in range(SLOTS - 1):
                start(col_copy(h, s), "col", h, s)
        else:
            col_out[1, h, slot_rows(0, 6)] = total[: 6 * part_rows].astype(BF16)
            for i in range(3):
                start(z_copy(h, i), "z", h, i)
            keep[h] = total[6 * part_rows : last]
        acc[b, h] -= total[last:]

    def first_residual(h):
        res = acc[0, h]
        for s in range(SLOTS - 1):
            arrive("col", h, s)
            res = res - col_in[0, h, slot_rows(s)].astype(F32)
        return res.astype(BF16)

    def second_sum_over_z(h):
        there, here = keep[h], acc[1, h]
        for i in range(3):
            arrive("z", h, i)
            there = there + col_in[1, h, slot_rows(2 * i)].astype(F32)
            here = here - col_in[1, h, slot_rows(2 * i + 1)].astype(F32)
        x_out[h] = there.astype(BF16)
        start(x_copy(h), "x", h)
        acc[1, h] = here

    def solve_copy(outgoing, incoming, sems, h, j):
        return remote(outgoing.at[h, j], incoming.at[h, row], sems.at[0, h, j], sems.at[1, h, row], (j, col))

    def solve_send(b, h, res, outgoing, incoming, sems):
        def group(js):
            for j in js:
                product = dot(res, inv_v[b, :, j * local_rows : (j + 1) * local_rows], NN)
                part[b, h, j] = product
                outgoing[h, j] = product.astype(BF16)
            for j in js:
                @pl.when(row < j)
                def _():
                    solve_copy(outgoing, incoming, sems, h, j).start()

        group(range(ROWS - 1, 3, -1))

        @pl.when(row < 4)
        def _():
            group(range(3, -1, -1))

        def drain():
            for j in range(1, ROWS):
                @pl.when(row < j)
                def _():
                    solve_copy(outgoing, incoming, sems, h, j).wait_send()

        def wait(i):
            pltpu.make_async_remote_copy(
                src_ref=incoming.at[h, i], dst_ref=incoming.at[h, i],
                send_sem=sems.at[0, h, i], recv_sem=sems.at[1, h, i],
                device_id=(row, col), device_id_type=MESH,
            ).wait_recv()

        def add(i):
            wait(i)
            part[b, h, row] += incoming[h, i].astype(F32)

        def receive():
            for i in range(ROWS - 2, -1, -1):
                pl.when(row > i)(functools.partial(add, i))

        drains.append(drain)
        arrivals["solve", b, h] = receive

    def solve_receive(b, h):
        arrive("solve", b, h)

        return part[b, h, row].astype(BF16)

    def f_copy(h, i):
        return remote(
            f_all.at[h, row], f_all.at[h, row], f_sem.at[0, h, i], f_sem.at[1, h, i],
            (lax.rem(row + i, ROWS), col),
        )

    def first_send(h):
        f_all[h, row] = solve_receive(0, h)
        for i in (6, 5, 7, 4, 3, 2, 1):
            start(f_copy(h, i), "f", h, i)

    def carry(h):
        arrive("x", h)
        res = acc[1, h] - x_in[h].astype(F32)

        def term(owner):
            at = pl.ds(pl.multiple_of(owner * local_rows, local_rows), local_rows)
            return dot(f_all[h, owner], lnk_v[:, at], NT)

        res = res - term(row)
        for i in (1, 7, 2, 6, 3, 5, 4):
            arrive("f", h, i)
            res = res - term(lax.rem(row + ROWS - i, ROWS))
        solve_send(1, h, res.astype(BF16), c_out, c_in, c_sem)

    def finish(h):
        second = solve_receive(1, h)
        both = jnp.stack([f_all[h, row].astype(F32), second.astype(F32)], axis=1)
        out[pl.ds(h * part_rows, part_rows)] = both.astype(BF16)

    def a_step(h):
        if h == 0:
            arrive("inverse", 0)
        solve_send(0, h, first_residual(h), a_out, a_in, a_sem)

    def carry_step(h):
        if h == 0:
            arrive("link")
            arrive("inverse", 1)
        carry(h)

    program = (
        lambda: sibling_part(0, 0), lambda: own_part(0, 0),
        lambda: sibling_part(0, 1), lambda: own_part(0, 1),
        lambda: sibling_part(1, 0), lambda: own_part(1, 0),
        lambda: sibling_part(1, 1),
        lambda: a_step(0),
        lambda: own_part(1, 1),
        lambda: a_step(1),
        lambda: first_send(0),
        lambda: second_sum_over_z(0), lambda: second_sum_over_z(1),
        lambda: first_send(1),
        lambda: carry_step(0), lambda: carry_step(1),
        lambda: finish(0), lambda: finish(1),
    )
    for step in program[:stages]:
        step()
    for wait in [*arrivals.values(), *drains]:
        wait()


def local(rhs, solved, panel, inverse, link, stages=None):
    samples, _, local_rows = rhs.shape
    part_rows = samples // HALVES
    piece = (part_rows, local_rows)
    column = (HALVES, SLOTS * part_rows, local_rows)
    any_spec = pl.BlockSpec(memory_space=pl.ANY)
    dma = pltpu.SemaphoreType.DMA
    return pl.pallas_call(
        functools.partial(kernel, stages),
        out_shape=jax.ShapeDtypeStruct(rhs.shape, BF16),
        in_specs=[any_spec] * 5,
        out_specs=pl.BlockSpec(memory_space=pltpu.VMEM),
        scratch_shapes=[
            pltpu.VMEM((2, HALVES, SLOTS * part_rows, solved.shape[1]), BF16),
            pltpu.VMEM(panel.shape, BF16),
            pltpu.VMEM(inverse.shape, BF16),
            pltpu.VMEM(link.shape, BF16),
            pltpu.VMEM(rhs.shape, BF16),
            pltpu.VMEM((2,) + column, BF16),
            pltpu.VMEM((2,) + column, BF16),
            pltpu.VMEM((2,) + column, BF16),
            pltpu.VMEM((2,) + column, BF16),
            pltpu.VMEM((HALVES,) + piece, BF16),
            pltpu.VMEM((HALVES,) + piece, BF16),
            pltpu.VMEM((HALVES,) + piece, F32),
            pltpu.VMEM((2, HALVES) + piece, F32),
            pltpu.VMEM((2, HALVES, ROWS) + piece, F32),
            pltpu.VMEM((HALVES, ROWS) + piece, BF16),
            pltpu.VMEM((HALVES, ROWS) + piece, BF16),
            pltpu.VMEM((HALVES, ROWS) + piece, BF16),
            pltpu.VMEM((HALVES, ROWS) + piece, BF16),
            pltpu.VMEM((HALVES, ROWS) + piece, BF16),
            dma((38,)),
            dma((2, 2, HALVES)),
            dma((2, 2, HALVES, SLOTS)),
            dma((2, HALVES)),
            dma((2, HALVES, ROWS)),
            dma((2, HALVES, ROWS)),
            dma((2, HALVES, ROWS)),
        ],
        compiler_params=pltpu.CompilerParams(
            collective_id=0 if stages is None else stages, has_side_effects=True, vmem_limit_bytes=56 << 20
        ),
        cost_estimate=pl.CostEstimate(
            flops=4 * solved.shape[0] * solved.shape[1] * local_rows, bytes_accessed=24 << 20, transcendentals=0
        ),
        name="window_solve" if stages is None else f"stage{stages:02d}",
    )(solved, panel, inverse, link, rhs)


def solution(mesh):
    return jax.shard_map(
        local,
        mesh=mesh,
        in_specs=(
            P("col", None, "row"),
            P(None, "col"),
            P(None, "row", "col"),
            P(None, "row", None),
            P("row", None),
        ),
        out_specs=P("col", None, "row"),
        check_vma=False,
    )
```

```python
import functools

import jax
import jax.numpy as jnp
from jax import lax
from jax.experimental import pallas as pl
from jax.experimental.pallas import tpu as pltpu
from jax.sharding import PartitionSpec as P

MESH = pl.DeviceIdType.MESH
BF16 = jnp.bfloat16
F32 = jnp.float32
NT = (((1,), (1,)), ((), ()))
NN = (((1,), (0,)), ((), ()))
ROWS = 8
SLOTS = 8
Z_OFFSETS = (2, 1, 3, 0)
HALVES = 2


def dot(left, right, dims):
    return lax.dot_general(left, right, dims, preferred_element_type=F32)


def kernel(
    stages, solved, panel, inverse, link, rhs, out,
    sol_v, pan_v, inv_v, lnk_v, rhs_v,
    core_out, core_in, col_out, col_in, x_out, x_in, keep, acc,
    part, a_out, a_in, f_all, c_out, c_in,
    load_sem, core_sem, col_sem, x_sem, a_sem, f_sem, c_sem,
):
    samples, local_rows = rhs.shape[0], rhs.shape[2]
    part_rows = samples // HALVES
    row, col = lax.axis_index("row"), lax.axis_index("col")
    x_lo = row // 4
    x_hi, z, core = col // 8, (col // 2) % 4, col % 2
    drains, arrivals = [], {}

    def col_of(dx, dz, k):
        return lax.rem(x_hi + dx, 2) * 8 + lax.rem(z + dz, 4) * 2 + k

    def remote(src, dst, send_sem, recv_sem, device):
        return pltpu.make_async_remote_copy(
            src_ref=src, dst_ref=dst, send_sem=send_sem, recv_sem=recv_sem,
            device_id=device, device_id_type=MESH,
        )

    def start(copy, *key):
        copy.start()
        drains.append(copy.wait_send)
        arrivals[key] = copy.wait_recv

    def arrive(*key):
        arrivals.pop(key)()

    def slot_of(s):
        return Z_OFFSETS[s // 2], 1 - s % 2

    def slot_rows(s, count=1):
        return pl.ds(s * part_rows, count * part_rows)

    def load_sol(kind, h, s):
        dz, dx = slot_of(s)
        c = col_of(dx, dz, 1 - core if kind == 0 else core)
        at = pl.multiple_of(c * samples + h * part_rows, part_rows)
        return pltpu.make_async_copy(
            solved.at[pl.ds(at, part_rows)], sol_v.at[kind, h, slot_rows(s)],
            load_sem.at[(kind * HALVES + h) * SLOTS + s],
        )

    load_panel = [pltpu.make_async_copy(panel.at[b], pan_v.at[b], load_sem.at[32 + b]) for b in range(2)]
    load_inv = [pltpu.make_async_copy(inverse.at[b], inv_v.at[b], load_sem.at[34 + b]) for b in range(2)]
    load_link = pltpu.make_async_copy(link, lnk_v, load_sem.at[36])
    load_rhs = pltpu.make_async_copy(rhs, rhs_v, load_sem.at[37])
    def load(copy, *key):
        copy.start()
        arrivals[key] = copy.wait

    def load_half(kind, h):
        for s in range(SLOTS):
            load(load_sol(kind, h, s), "sol", kind, h, s)

    load(load_panel[0], "panel", 0)
    load_half(0, 0)
    load_half(1, 0)
    load(load_rhs, "rhs")
    load_half(0, 1)
    load_half(1, 1)

    barrier = pltpu.get_barrier_semaphore()
    for i in range(1, ROWS):
        pl.semaphore_signal(barrier, inc=1, device_id=(lax.rem(row + i, ROWS), col), device_id_type=MESH)
    for s in range(SLOTS - 1):
        dz, dx = slot_of(s)
        pl.semaphore_signal(barrier, inc=1, device_id=(row, col_of(dx, dz, core)), device_id_type=MESH)
    sibling = (row, col_of(0, 0, 1 - core))
    pl.semaphore_signal(barrier, inc=1, device_id=sibling, device_id_type=MESH)

    def take_rhs():
        arrive("rhs")
        rhs_all = rhs_v[...].astype(F32)
        for b in range(2):
            for h in range(HALVES):
                acc[b, h] = rhs_all[h * part_rows : (h + 1) * part_rows, b, :]

    def core_copy(b, h):
        return remote(core_out.at[b, h], core_in.at[b, h], core_sem.at[0, b, h], core_sem.at[1, b, h], sibling)

    def col_copy(h, s):
        dz, dx = slot_of(s)
        return remote(
            col_out.at[0, h, slot_rows(s)], col_in.at[0, h, slot_rows(s)],
            col_sem.at[0, 0, h, s], col_sem.at[1, 0, h, s], (row, col_of(dx, dz, core)),
        )

    def z_copy(h, i):
        at = slot_rows(2 * i, 2)
        return remote(
            col_out.at[1, h, at], col_in.at[1, h, at],
            col_sem.at[0, 1, h, i], col_sem.at[1, 1, h, i], (row, col_of(0, Z_OFFSETS[i], core)),
        )

    def x_copy(h):
        return remote(x_out.at[h], x_in.at[h], x_sem.at[0, h], x_sem.at[1, h], (row, col_of(1, 0, core)))

    def sibling_part(b, h):
        if b == 0:
            for s in range(SLOTS):
                arrive("sol", 0, h, s)
        if h == 0:
            arrive("panel", b)
        if (b, h) == (0, 1):
            load(load_panel[1], "panel", 1)
            load(load_inv[0], "inverse", 0)
        core_out[b, h] = dot(sol_v[0, h], pan_v[b], NT).astype(BF16)
        if (b, h) == (0, 0):
            pl.semaphore_wait(barrier, 15)
        start(core_copy(b, h), "core", b, h)

    def own_part(b, h):
        if b == 0:
            for s in range(SLOTS):
                arrive("sol", 1, h, s)
        if (b, h) == (1, 0):
            load(load_link, "link")
            load(load_inv[1], "inverse", 1)
        total = dot(sol_v[1, h], pan_v[b], NT)
        if (b, h) == (0, 0):
            clear()
            take_rhs()
        arrive("core", b, h)
        total = total + core_in[b, h].astype(F32)
        last = 7 * part_rows
        if b == 0:
            col_out[0, h, slot_rows(0, 7)] = total[:last].astype(BF16)
            for s in range(SLOTS - 1):
                start(col_copy(h, s), "col", h, s)
        else:
            col_out[1, h, slot_rows(0, 6)] = total[: 6 * part_rows].astype(BF16)
            for i in range(3):
                start(z_copy(h, i), "z", h, i)
            keep[h] = total[6 * part_rows : last]
        acc[b, h] -= total[last:]

    def first_residual(h):
        for s in range(SLOTS - 1):
            arrive("col", h, s)
        res = acc[0, h]
        for s in range(SLOTS - 1):
            res = res - col_in[0, h, slot_rows(s)].astype(F32)
        return res.astype(BF16)

    def second_sum_over_z(h):
        for i in range(3):
            arrive("z", h, i)
        there, here = keep[h], acc[1, h]
        for i in range(3):
            there = there + col_in[1, h, slot_rows(2 * i)].astype(F32)
            here = here - col_in[1, h, slot_rows(2 * i + 1)].astype(F32)
        x_out[h] = there.astype(BF16)
        start(x_copy(h), "x", h)
        acc[1, h] = here

    def solve_copy(outgoing, incoming, sems, h, j):
        return remote(outgoing.at[h, j], incoming.at[h, row], sems.at[0, h, j], sems.at[1, h, row], (j, col))

    def solve_send(b, h, res, outgoing, incoming, sems):
        def group(js):
            for j in js:
                product = dot(res, inv_v[b, :, j * local_rows : (j + 1) * local_rows], NN)
                part[b, h, j] = product
                outgoing[h, j] = product.astype(BF16)
            for j in js:
                @pl.when(row < j)
                def _():
                    solve_copy(outgoing, incoming, sems, h, j).start()

        group(range(ROWS - 1, 3, -1))

        @pl.when(row < 4)
        def _():
            group(range(3, -1, -1))

        def drain():
            for j in range(1, ROWS):
                @pl.when(row < j)
                def _():
                    solve_copy(outgoing, incoming, sems, h, j).wait_send()

        def wait(i):
            pltpu.make_async_remote_copy(
                src_ref=incoming.at[h, i], dst_ref=incoming.at[h, i],
                send_sem=sems.at[0, h, i], recv_sem=sems.at[1, h, i],
                device_id=(row, col), device_id_type=MESH,
            ).wait_recv()

        def receive():
            for i in range(ROWS - 1):
                pl.when(row > i)(functools.partial(wait, i))

        drains.append(drain)
        arrivals["solve", b, h] = receive

    def solve_receive(b, h, incoming):
        arrive("solve", b, h)
        total = part[b, h, row]
        for i in range(ROWS - 1):
            total = total + incoming[h, i].astype(F32)
        return total.astype(BF16)

    def clear():
        for i in range(ROWS - 1):
            @pl.when(row <= i)
            def _():
                a_in[:, i] = jnp.zeros_like(a_in[:, i])
                c_in[:, i] = jnp.zeros_like(c_in[:, i])

    def f_copy(h, i):
        return remote(
            f_all.at[h, row], f_all.at[h, row], f_sem.at[0, h, i], f_sem.at[1, h, row],
            (lax.rem(row + i, ROWS), col),
        )

    def f_wait(h, owner):
        remote(
            f_all.at[h, owner], f_all.at[h, owner], f_sem.at[0, h, owner], f_sem.at[1, h, owner], (row, col)
        ).wait_recv()

    def first_send(h):
        f_all[h, row] = solve_receive(0, h, a_in)
        for i in (6, 5, 7, 4, 3, 2, 1):
            copy = f_copy(h, i)
            copy.start()
            drains.append(copy.wait_send)

        def receive():
            for owner in range(ROWS):
                pl.when(row != owner)(functools.partial(f_wait, h, owner))

        arrivals["f", h] = receive

    def carry(h):
        arrivals.pop(("f", h))
        arrive("x", h)
        res = acc[1, h] - x_in[h].astype(F32)

        def term(owner):
            at = pl.ds(pl.multiple_of(owner * local_rows, local_rows), local_rows)
            return dot(f_all[h, owner], lnk_v[:, at], NT)

        for other in range(2):
            base = lax.rem(x_lo + other, 2) * 4
            for i in range(4):
                @pl.when(base + i != row)
                def _():
                    f_wait(h, base + i)
            res = res - sum(term(base + i) for i in range(4))
        solve_send(1, h, res.astype(BF16), c_out, c_in, c_sem)

    def finish(h):
        second = solve_receive(1, h, c_in)
        both = jnp.stack([f_all[h, row].astype(F32), second.astype(F32)], axis=1)
        out[pl.ds(h * part_rows, part_rows)] = both.astype(BF16)

    def a_step(h):
        if h == 0:
            arrive("inverse", 0)
        solve_send(0, h, first_residual(h), a_out, a_in, a_sem)

    def carry_step(h):
        if h == 0:
            arrive("link")
            arrive("inverse", 1)
        carry(h)

    program = (
        lambda: sibling_part(0, 0), lambda: own_part(0, 0),
        lambda: sibling_part(0, 1), lambda: own_part(0, 1),
        lambda: sibling_part(1, 0), lambda: own_part(1, 0),
        lambda: a_step(0),
        lambda: sibling_part(1, 1),
        lambda: a_step(1),
        lambda: own_part(1, 1),
        lambda: first_send(0),
        lambda: second_sum_over_z(0),
        lambda: first_send(1),
        lambda: second_sum_over_z(1),
        lambda: carry_step(0), lambda: carry_step(1),
        lambda: finish(0), lambda: finish(1),
    )
    for step in program[:stages]:
        step()
    for wait in [*arrivals.values(), *drains]:
        wait()


def local(rhs, solved, panel, inverse, link, stages=None):
    samples, _, local_rows = rhs.shape
    part_rows = samples // HALVES
    piece = (part_rows, local_rows)
    column = (HALVES, SLOTS * part_rows, local_rows)
    any_spec = pl.BlockSpec(memory_space=pl.ANY)
    dma = pltpu.SemaphoreType.DMA
    return pl.pallas_call(
        functools.partial(kernel, stages),
        out_shape=pltpu.VMEM(rhs.shape, BF16),
        in_specs=[any_spec] * 5,
        out_specs=pl.BlockSpec(memory_space=pltpu.VMEM),
        scratch_shapes=[
            pltpu.VMEM((2, HALVES, SLOTS * part_rows, solved.shape[1]), BF16),
            pltpu.VMEM(panel.shape, BF16),
            pltpu.VMEM(inverse.shape, BF16),
            pltpu.VMEM(link.shape, BF16),
            pltpu.VMEM(rhs.shape, BF16),
            pltpu.VMEM((2,) + column, BF16),
            pltpu.VMEM((2,) + column, BF16),
            pltpu.VMEM((2,) + column, BF16),
            pltpu.VMEM((2,) + column, BF16),
            pltpu.VMEM((HALVES,) + piece, BF16),
            pltpu.VMEM((HALVES,) + piece, BF16),
            pltpu.VMEM((HALVES,) + piece, F32),
            pltpu.VMEM((2, HALVES) + piece, F32),
            pltpu.VMEM((2, HALVES, ROWS) + piece, F32),
            pltpu.VMEM((HALVES, ROWS) + piece, BF16),
            pltpu.VMEM((HALVES, ROWS) + piece, BF16),
            pltpu.VMEM((HALVES, ROWS) + piece, BF16),
            pltpu.VMEM((HALVES, ROWS) + piece, BF16),
            pltpu.VMEM((HALVES, ROWS) + piece, BF16),
            dma((38,)),
            dma((2, 2, HALVES)),
            dma((2, 2, HALVES, SLOTS)),
            dma((2, HALVES)),
            dma((2, HALVES, ROWS)),
            dma((2, HALVES, ROWS)),
            dma((2, HALVES, ROWS)),
        ],
        compiler_params=pltpu.CompilerParams(
            collective_id=0 if stages is None else stages, has_side_effects=True, vmem_limit_bytes=56 << 20
        ),
        cost_estimate=pl.CostEstimate(
            flops=4 * solved.shape[0] * solved.shape[1] * local_rows, bytes_accessed=24 << 20, transcendentals=0
        ),
        name="window_solve" if stages is None else f"stage{stages:02d}",
    )(solved, panel, inverse, link, rhs)


def solution(mesh):
    return jax.shard_map(
        local,
        mesh=mesh,
        in_specs=(
            P("col", None, "row"),
            P(None, "col"),
            P(None, "row", "col"),
            P(None, "row", None),
            P("row", None),
        ),
        out_specs=P("col", None, "row"),
        check_vma=False,
    )
```

```python
import functools

import jax
import jax.numpy as jnp
from jax import lax
from jax.experimental import pallas as pl
from jax.experimental.pallas import tpu as pltpu
from jax.sharding import PartitionSpec as P

MESH = pl.DeviceIdType.MESH
BF16 = jnp.bfloat16
F32 = jnp.float32
NT = (((1,), (1,)), ((), ()))
NN = (((1,), (0,)), ((), ()))
ROWS = 8
SLOTS = 8
Z_OFFSETS = (2, 1, 3, 0)
HALVES = 2


def dot(left, right, dims):
    return lax.dot_general(left, right, dims, preferred_element_type=F32)


def kernel(
    stages, solved, panel, inverse, link, rhs, out,
    sol_v, pan_v, inv_v, lnk_v, rhs_v,
    core_out, core_in, own, col_out, col_in, x_out, x_in, keep, acc,
    part, a_out, a_in, f_all, c_out, c_in,
    load_sem, core_sem, col_sem, x_sem, a_sem, f_sem, c_sem,
):
    samples, local_rows = rhs.shape[0], rhs.shape[2]
    part_rows = samples // HALVES
    row, col = lax.axis_index("row"), lax.axis_index("col")
    x_lo = row // 4
    x_hi, z, core = col // 8, (col // 2) % 4, col % 2
    drains, arrivals = [], {}

    def col_of(dx, dz, k):
        return lax.rem(x_hi + dx, 2) * 8 + lax.rem(z + dz, 4) * 2 + k

    def remote(src, dst, send_sem, recv_sem, device):
        return pltpu.make_async_remote_copy(
            src_ref=src, dst_ref=dst, send_sem=send_sem, recv_sem=recv_sem,
            device_id=device, device_id_type=MESH,
        )

    def start(copy, *key):
        copy.start()
        drains.append(copy.wait_send)
        arrivals[key] = copy.wait_recv

    def arrive(*key):
        arrivals.pop(key)()

    def slot_of(s):
        return Z_OFFSETS[s // 2], 1 - s % 2

    def slot_rows(s, count=1):
        return pl.ds(s * part_rows, count * part_rows)

    def load_sol(kind, h, s):
        dz, dx = slot_of(s)
        c = col_of(dx, dz, 1 - core if kind == 0 else core)
        at = pl.multiple_of(c * samples + h * part_rows, part_rows)
        return pltpu.make_async_copy(
            solved.at[pl.ds(at, part_rows)], sol_v.at[kind, h, slot_rows(s)],
            load_sem.at[(kind * HALVES + h) * SLOTS + s],
        )

    load_panel = [pltpu.make_async_copy(panel.at[b], pan_v.at[b], load_sem.at[32 + b]) for b in range(2)]
    load_inv = [pltpu.make_async_copy(inverse.at[b], inv_v.at[b], load_sem.at[34 + b]) for b in range(2)]
    load_link = pltpu.make_async_copy(link, lnk_v, load_sem.at[36])
    load_rhs = pltpu.make_async_copy(rhs, rhs_v, load_sem.at[37])
    def load(copy, *key):
        copy.start()
        arrivals[key] = copy.wait

    def load_half(kind, h):
        for s in range(SLOTS):
            load(load_sol(kind, h, s), "sol", kind, h, s)

    load(load_panel[0], "panel", 0)
    load_half(0, 0)
    load_half(1, 0)
    load(load_rhs, "rhs")
    load_half(0, 1)
    load_half(1, 1)

    barrier = pltpu.get_barrier_semaphore()
    for i in range(1, ROWS):
        pl.semaphore_signal(barrier, inc=1, device_id=(lax.rem(row + i, ROWS), col), device_id_type=MESH)
    for s in range(SLOTS - 1):
        dz, dx = slot_of(s)
        pl.semaphore_signal(barrier, inc=1, device_id=(row, col_of(dx, dz, core)), device_id_type=MESH)
    sibling = (row, col_of(0, 0, 1 - core))
    pl.semaphore_signal(barrier, inc=1, device_id=sibling, device_id_type=MESH)

    def take_rhs():
        arrive("rhs")
        rhs_all = rhs_v[...].astype(F32)
        for b in range(2):
            for h in range(HALVES):
                acc[b, h] = rhs_all[h * part_rows : (h + 1) * part_rows, b, :]

    def core_copy(b, h):
        return remote(core_out.at[b, h], core_in.at[b, h], core_sem.at[0, b, h], core_sem.at[1, b, h], sibling)

    def col_copy(h, s):
        dz, dx = slot_of(s)
        return remote(
            col_out.at[0, h, slot_rows(s)], col_in.at[0, h, slot_rows(s)],
            col_sem.at[0, 0, h, s], col_sem.at[1, 0, h, s], (row, col_of(dx, dz, core)),
        )

    def z_copy(h, i):
        at = slot_rows(2 * i, 2)
        return remote(
            col_out.at[1, h, at], col_in.at[1, h, at],
            col_sem.at[0, 1, h, i], col_sem.at[1, 1, h, i], (row, col_of(0, Z_OFFSETS[i], core)),
        )

    def x_copy(h):
        return remote(x_out.at[h], x_in.at[h], x_sem.at[0, h], x_sem.at[1, h], (row, col_of(1, 0, core)))

    def sibling_part(b, h):
        if b == 0:
            for s in range(SLOTS):
                arrive("sol", 0, h, s)
        if h == 0:
            arrive("panel", b)
        if (b, h) == (0, 1):
            load(load_panel[1], "panel", 1)
            load(load_inv[0], "inverse", 0)
        core_out[b, h] = dot(sol_v[0, h], pan_v[b], NT).astype(BF16)
        if (b, h) == (0, 0):
            pl.semaphore_wait(barrier, 15)
        start(core_copy(b, h), "core", b, h)

    def own_part(b, h):
        if b == 0:
            for s in range(SLOTS):
                arrive("sol", 1, h, s)
        if (b, h) == (0, 1):
            load(load_link, "link")
            load(load_inv[1], "inverse", 1)
        own[...] = dot(sol_v[1, h], pan_v[b], NT)

    def add_sibling(b, h):
        arrive("core", b, h)
        last = 7 * part_rows
        if b == 0:
            col_out[0, h, slot_rows(0, 7)] = (own[:last] + core_in[0, h, :last].astype(F32)).astype(BF16)
            for s in range(SLOTS - 1):
                start(col_copy(h, s), "col", h, s)
        else:
            sent = 6 * part_rows
            col_out[1, h, slot_rows(0, 6)] = (own[:sent] + core_in[1, h, :sent].astype(F32)).astype(BF16)
            keep[h] = own[sent:last] + core_in[1, h, sent:last].astype(F32)
        if (b, h) == (0, 0):
            clear()
            take_rhs()
        acc[b, h] -= own[last:] + core_in[b, h, last:].astype(F32)

    def z_send(h):
        for i in range(3):
            start(z_copy(h, i), "z", h, i)

    def first_residual(h):
        for s in range(SLOTS - 1):
            arrive("col", h, s)
        res = acc[0, h]
        for s in range(SLOTS - 1):
            res = res - col_in[0, h, slot_rows(s)].astype(F32)
        return res.astype(BF16)

    def second_sum_over_z(h):
        for i in range(3):
            arrive("z", h, i)
        there, here = keep[h], acc[1, h]
        for i in range(3):
            there = there + col_in[1, h, slot_rows(2 * i)].astype(F32)
            here = here - col_in[1, h, slot_rows(2 * i + 1)].astype(F32)
        x_out[h] = there.astype(BF16)
        start(x_copy(h), "x", h)
        acc[1, h] = here

    def solve_copy(outgoing, incoming, sems, h, j):
        return remote(outgoing.at[h, j], incoming.at[h, row], sems.at[0, h, j], sems.at[1, h, row], (j, col))

    def solve_send(b, h, res, outgoing, incoming, sems):
        def group(js):
            for j in js:
                product = dot(res, inv_v[b, :, j * local_rows : (j + 1) * local_rows], NN)
                part[b, h, j] = product
                outgoing[h, j] = product.astype(BF16)
            for j in js:
                @pl.when(row < j)
                def _():
                    solve_copy(outgoing, incoming, sems, h, j).start()

        group(range(ROWS - 1, 3, -1))

        @pl.when(row < 4)
        def _():
            group(range(3, -1, -1))

        def drain():
            for j in range(1, ROWS):
                @pl.when(row < j)
                def _():
                    solve_copy(outgoing, incoming, sems, h, j).wait_send()

        def wait(i):
            pltpu.make_async_remote_copy(
                src_ref=incoming.at[h, i], dst_ref=incoming.at[h, i],
                send_sem=sems.at[0, h, i], recv_sem=sems.at[1, h, i],
                device_id=(row, col), device_id_type=MESH,
            ).wait_recv()

        def receive():
            for i in range(ROWS - 1):
                pl.when(row > i)(functools.partial(wait, i))

        drains.append(drain)
        arrivals["solve", b, h] = receive

    def solve_receive(b, h, incoming):
        arrive("solve", b, h)
        total = part[b, h, row]
        for i in range(ROWS - 1):
            total = total + incoming[h, i].astype(F32)
        return total.astype(BF16)

    def clear():
        for i in range(ROWS - 1):
            @pl.when(row <= i)
            def _():
                a_in[:, i] = jnp.zeros_like(a_in[:, i])
                c_in[:, i] = jnp.zeros_like(c_in[:, i])

    def f_copy(h, i):
        return remote(
            f_all.at[h, row], f_all.at[h, row], f_sem.at[0, h, i], f_sem.at[1, h, row],
            (lax.rem(row + i, ROWS), col),
        )

    def f_wait(h, owner):
        remote(
            f_all.at[h, owner], f_all.at[h, owner], f_sem.at[0, h, owner], f_sem.at[1, h, owner], (row, col)
        ).wait_recv()

    def first_send(h):
        f_all[h, row] = solve_receive(0, h, a_in)
        for i in (6, 5, 7, 4, 3, 2, 1):
            copy = f_copy(h, i)
            copy.start()
            drains.append(copy.wait_send)

        def receive():
            for owner in range(ROWS):
                pl.when(row != owner)(functools.partial(f_wait, h, owner))

        arrivals["f", h] = receive

    def carry(h):
        arrivals.pop(("f", h))
        arrive("x", h)
        res = acc[1, h] - x_in[h].astype(F32)

        def term(owner):
            at = pl.ds(pl.multiple_of(owner * local_rows, local_rows), local_rows)
            return dot(f_all[h, owner], lnk_v[:, at], NT)

        y = lax.rem(row, 4)
        for other, steps in ((0, (0, 1, 3, 2)), (1, (0, 1)), (1, (3, 2))):
            owners = [lax.rem(x_lo + other, 2) * 4 + lax.rem(y + step, 4) for step in steps]
            for owner, step in zip(owners, steps):
                if other or step:
                    f_wait(h, owner)
            res = res - sum(term(owner) for owner in owners)
        solve_send(1, h, res.astype(BF16), c_out, c_in, c_sem)

    def finish(h):
        second = solve_receive(1, h, c_in)
        both = jnp.stack([f_all[h, row].astype(F32), second.astype(F32)], axis=1)
        out[pl.ds(h * part_rows, part_rows)] = both.astype(BF16)

    def a_step(h):
        if h == 0:
            arrive("inverse", 0)
        solve_send(0, h, first_residual(h), a_out, a_in, a_sem)

    def carry_step(h):
        if h == 0:
            arrive("link")
            arrive("inverse", 1)
        carry(h)

    program = (
        lambda: sibling_part(0, 0), lambda: own_part(0, 0),
        lambda: sibling_part(0, 1), lambda: add_sibling(0, 0), lambda: own_part(0, 1),
        lambda: sibling_part(1, 0), lambda: add_sibling(0, 1), lambda: own_part(1, 0),
        lambda: sibling_part(1, 1), lambda: add_sibling(1, 0),
        lambda: own_part(1, 1),
        lambda: a_step(0),
        lambda: z_send(0), lambda: add_sibling(1, 1),
        lambda: a_step(1),
        lambda: z_send(1),
        lambda: first_send(0),
        lambda: second_sum_over_z(0),
        lambda: first_send(1),
        lambda: second_sum_over_z(1),
        lambda: carry_step(0), lambda: carry_step(1),
        lambda: finish(0), lambda: finish(1),
    )
    for step in program[:stages]:
        step()
    for wait in [*arrivals.values(), *drains]:
        wait()


def local(rhs, solved, panel, inverse, link, stages=None):
    samples, _, local_rows = rhs.shape
    part_rows = samples // HALVES
    piece = (part_rows, local_rows)
    column = (HALVES, SLOTS * part_rows, local_rows)
    any_spec = pl.BlockSpec(memory_space=pl.ANY)
    dma = pltpu.SemaphoreType.DMA
    return pl.pallas_call(
        functools.partial(kernel, stages),
        out_shape=pltpu.VMEM(rhs.shape, BF16),
        in_specs=[any_spec] * 5,
        out_specs=pl.BlockSpec(memory_space=pltpu.VMEM),
        scratch_shapes=[
            pltpu.VMEM((2, HALVES, SLOTS * part_rows, solved.shape[1]), BF16),
            pltpu.VMEM(panel.shape, BF16),
            pltpu.VMEM(inverse.shape, BF16),
            pltpu.VMEM(link.shape, BF16),
            pltpu.VMEM(rhs.shape, BF16),
            pltpu.VMEM((2,) + column, BF16),
            pltpu.VMEM((2,) + column, BF16),
            pltpu.VMEM((SLOTS * part_rows, local_rows), F32),
            pltpu.VMEM((2,) + column, BF16),
            pltpu.VMEM((2,) + column, BF16),
            pltpu.VMEM((HALVES,) + piece, BF16),
            pltpu.VMEM((HALVES,) + piece, BF16),
            pltpu.VMEM((HALVES,) + piece, F32),
            pltpu.VMEM((2, HALVES) + piece, F32),
            pltpu.VMEM((2, HALVES, ROWS) + piece, F32),
            pltpu.VMEM((HALVES, ROWS) + piece, BF16),
            pltpu.VMEM((HALVES, ROWS) + piece, BF16),
            pltpu.VMEM((HALVES, ROWS) + piece, BF16),
            pltpu.VMEM((HALVES, ROWS) + piece, BF16),
            pltpu.VMEM((HALVES, ROWS) + piece, BF16),
            dma((38,)),
            dma((2, 2, HALVES)),
            dma((2, 2, HALVES, SLOTS)),
            dma((2, HALVES)),
            dma((2, HALVES, ROWS)),
            dma((2, HALVES, ROWS)),
            dma((2, HALVES, ROWS)),
        ],
        compiler_params=pltpu.CompilerParams(
            collective_id=0 if stages is None else stages, has_side_effects=True, vmem_limit_bytes=56 << 20
        ),
        cost_estimate=pl.CostEstimate(
            flops=4 * solved.shape[0] * solved.shape[1] * local_rows, bytes_accessed=24 << 20, transcendentals=0
        ),
        name="window_solve" if stages is None else f"stage{stages:02d}",
    )(solved, panel, inverse, link, rhs)


def solution(mesh):
    return jax.shard_map(
        local,
        mesh=mesh,
        in_specs=(
            P("col", None, "row"),
            P(None, "col"),
            P(None, "row", "col"),
            P(None, "row", None),
            P("row", None),
        ),
        out_specs=P("col", None, "row"),
        check_vma=False,
    )
```

```python
import functools

import jax
import jax.numpy as jnp
from jax import lax
from jax.experimental import pallas as pl
from jax.experimental.pallas import tpu as pltpu
from jax.sharding import PartitionSpec as P

MESH = pl.DeviceIdType.MESH
BF16 = jnp.bfloat16
F32 = jnp.float32
NT = (((1,), (1,)), ((), ()))
NN = (((1,), (0,)), ((), ()))
ROWS = 8
F_ORDER = ((1, 2), (1, 1), (1, 3), (0, 2), (1, 0), (0, 1), (0, 3))
SLOTS = 8
Y_OFFSETS = Z_OFFSETS = (2, 1, 3, 0)
HALVES = 2


def dot(left, right, dims):
    return lax.dot_general(left, right, dims, preferred_element_type=F32)


def kernel(
    stages, solved, panel, inverse, link, rhs, out,
    sol_v, pan_v, inv_v, lnk_v, rhs_v,
    core_out, core_in, own, col_out, col_in, x_out, x_in, keep, acc,
    part, a_out, a_in, f_all, c_out, c_in,
    load_sem, core_sem, col_sem, x_sem, a_sem, f_sem, c_sem,
):
    samples, local_rows = rhs.shape[0], rhs.shape[2]
    part_rows = samples // HALVES
    row, col = lax.axis_index("row"), lax.axis_index("col")
    x_lo, y = row // 4, row % 4
    x_hi, z, core = col // 8, (col // 2) % 4, col % 2
    drains, arrivals = [], {}

    def col_of(dx, dz, k):
        return lax.rem(x_hi + dx, 2) * 8 + lax.rem(z + dz, 4) * 2 + k

    def remote(src, dst, send_sem, recv_sem, device):
        return pltpu.make_async_remote_copy(
            src_ref=src, dst_ref=dst, send_sem=send_sem, recv_sem=recv_sem,
            device_id=device, device_id_type=MESH,
        )

    def start(copy, *key):
        copy.start()
        drains.append(copy.wait_send)
        arrivals[key] = copy.wait_recv

    def arrive(*key):
        arrivals.pop(key)()

    def slot_of(s):
        return Z_OFFSETS[s // 2], 1 - s % 2

    def slot_rows(s, count=1):
        return pl.ds(s * part_rows, count * part_rows)

    def load_sol(kind, h, s):
        dz, dx = slot_of(s)
        c = col_of(dx, dz, 1 - core if kind == 0 else core)
        at = pl.multiple_of(c * samples + h * part_rows, part_rows)
        return pltpu.make_async_copy(
            solved.at[pl.ds(at, part_rows)], sol_v.at[kind, h, slot_rows(s)],
            load_sem.at[(kind * HALVES + h) * SLOTS + s],
        )

    load_panel = [pltpu.make_async_copy(panel.at[b], pan_v.at[b], load_sem.at[32 + b]) for b in range(2)]
    load_inv = [pltpu.make_async_copy(inverse.at[b], inv_v.at[b], load_sem.at[34 + b]) for b in range(2)]
    load_link = pltpu.make_async_copy(link, lnk_v, load_sem.at[36])
    load_rhs = pltpu.make_async_copy(rhs, rhs_v, load_sem.at[37])
    def load(copy, *key):
        copy.start()
        arrivals[key] = copy.wait

    def load_half(kind, h):
        for s in range(SLOTS):
            load(load_sol(kind, h, s), "sol", kind, h, s)

    load(load_panel[0], "panel", 0)
    load_half(0, 0)
    load_half(1, 0)
    load(load_rhs, "rhs")
    load_half(0, 1)
    load_half(1, 1)

    barrier = pltpu.get_barrier_semaphore()
    for i in range(1, ROWS):
        pl.semaphore_signal(barrier, inc=1, device_id=(lax.rem(row + i, ROWS), col), device_id_type=MESH)
    for s in range(SLOTS - 1):
        dz, dx = slot_of(s)
        pl.semaphore_signal(barrier, inc=1, device_id=(row, col_of(dx, dz, core)), device_id_type=MESH)
    sibling = (row, col_of(0, 0, 1 - core))
    pl.semaphore_signal(barrier, inc=1, device_id=sibling, device_id_type=MESH)

    def take_rhs():
        arrive("rhs")
        rhs_all = rhs_v[...].astype(F32)
        for b in range(2):
            for h in range(HALVES):
                acc[b, h] = rhs_all[h * part_rows : (h + 1) * part_rows, b, :]

    def core_copy(b, h):
        return remote(core_out.at[b, h], core_in.at[b, h], core_sem.at[0, b, h], core_sem.at[1, b, h], sibling)

    def col_copy(h, s):
        dz, dx = slot_of(s)
        return remote(
            col_out.at[0, h, slot_rows(s)], col_in.at[0, h, slot_rows(s)],
            col_sem.at[0, 0, h, s], col_sem.at[1, 0, h, s], (row, col_of(dx, dz, core)),
        )

    def z_copy(h, i):
        at = slot_rows(2 * i, 2)
        return remote(
            col_out.at[1, h, at], col_in.at[1, h, at],
            col_sem.at[0, 1, h, i], col_sem.at[1, 1, h, i], (row, col_of(0, Z_OFFSETS[i], core)),
        )

    def x_copy(h):
        return remote(x_out.at[h], x_in.at[h], x_sem.at[0, h], x_sem.at[1, h], (row, col_of(1, 0, core)))

    def sibling_part(b, h):
        if b == 0:
            for s in range(SLOTS):
                arrive("sol", 0, h, s)
        if h == 0:
            arrive("panel", b)
        if (b, h) == (0, 1):
            load(load_panel[1], "panel", 1)
            load(load_inv[0], "inverse", 0)
        core_out[b, h] = dot(sol_v[0, h], pan_v[b], NT).astype(BF16)
        if (b, h) == (0, 0):
            pl.semaphore_wait(barrier, 15)
        start(core_copy(b, h), "core", b, h)

    def own_part(b, h):
        if b == 0:
            for s in range(SLOTS):
                arrive("sol", 1, h, s)
        if (b, h) == (0, 1):
            load(load_link, "link")
            load(load_inv[1], "inverse", 1)
        own[...] = dot(sol_v[1, h], pan_v[b], NT)

    def add_sibling(b, h):
        arrive("core", b, h)
        last = 7 * part_rows
        if b == 0:
            col_out[0, h, slot_rows(0, 7)] = (own[:last] + core_in[0, h, :last].astype(F32)).astype(BF16)
            for s in range(SLOTS - 1):
                start(col_copy(h, s), "col", h, s)
        else:
            sent = 6 * part_rows
            col_out[1, h, slot_rows(0, 6)] = (own[:sent] + core_in[1, h, :sent].astype(F32)).astype(BF16)
            keep[h] = own[sent:last] + core_in[1, h, sent:last].astype(F32)
        if (b, h) == (0, 0):
            clear()
            take_rhs()
        acc[b, h] -= own[last:] + core_in[b, h, last:].astype(F32)

    def z_send(h):
        for i in range(3):
            start(z_copy(h, i), "z", h, i)

    def first_residual(h):
        for s in range(SLOTS - 1):
            arrive("col", h, s)
        res = acc[0, h]
        for s in range(SLOTS - 1):
            res = res - col_in[0, h, slot_rows(s)].astype(F32)
        return res.astype(BF16)

    def second_sum_over_z(h):
        for i in range(3):
            arrive("z", h, i)
        there, here = keep[h], acc[1, h]
        for i in range(3):
            there = there + col_in[1, h, slot_rows(2 * i)].astype(F32)
            here = here - col_in[1, h, slot_rows(2 * i + 1)].astype(F32)
        x_out[h] = there.astype(BF16)
        start(x_copy(h), "x", h)
        acc[1, h] = here

    def solve_copy(outgoing, incoming, sems, h, j):
        return remote(outgoing.at[h, j], incoming.at[h, row], sems.at[0, h, j], sems.at[1, h, row], (j, col))

    def solve_send(b, h, res, outgoing, incoming, sems):
        def group(base):
            for j in range(4 * base, 4 * base + 4):
                product = dot(res, inv_v[b, :, j * local_rows : (j + 1) * local_rows], NN)
                part[b, h, j] = product
                outgoing[h, j] = product.astype(BF16)
            for dy in Y_OFFSETS:
                j = 4 * base + lax.rem(y + dy, 4)

                @pl.when(row < j)
                def _():
                    solve_copy(outgoing, incoming, sems, h, j).start()

        group(1)

        @pl.when(row < 4)
        def _():
            group(0)

        def drain():
            for j in range(1, ROWS):
                @pl.when(row < j)
                def _():
                    solve_copy(outgoing, incoming, sems, h, j).wait_send()

        def wait(i):
            pltpu.make_async_remote_copy(
                src_ref=incoming.at[h, i], dst_ref=incoming.at[h, i],
                send_sem=sems.at[0, h, i], recv_sem=sems.at[1, h, i],
                device_id=(row, col), device_id_type=MESH,
            ).wait_recv()

        def receive():
            for i in range(ROWS - 1):
                pl.when(row > i)(functools.partial(wait, i))

        drains.append(drain)
        arrivals["solve", b, h] = receive

    def solve_receive(b, h, incoming):
        arrive("solve", b, h)
        total = part[b, h, row]
        for i in range(ROWS - 1):
            total = total + incoming[h, i].astype(F32)
        return total.astype(BF16)

    def clear():
        for i in range(ROWS - 1):
            @pl.when(row <= i)
            def _():
                a_in[:, i] = jnp.zeros_like(a_in[:, i])
                c_in[:, i] = jnp.zeros_like(c_in[:, i])

    def f_copy(h, i):
        dx, dy = F_ORDER[i]
        return remote(
            f_all.at[h, row], f_all.at[h, row], f_sem.at[0, h, i], f_sem.at[1, h, row],
            (lax.rem(x_lo + dx, 2) * 4 + lax.rem(y + dy, 4), col),
        )

    def f_wait(h, owner):
        remote(
            f_all.at[h, owner], f_all.at[h, owner], f_sem.at[0, h, owner], f_sem.at[1, h, owner], (row, col)
        ).wait_recv()

    def first_send(h):
        f_all[h, row] = solve_receive(0, h, a_in)
        for i in range(ROWS - 1):
            copy = f_copy(h, i)
            copy.start()
            drains.append(copy.wait_send)

        def receive():
            for owner in range(ROWS):
                pl.when(row != owner)(functools.partial(f_wait, h, owner))

        arrivals["f", h] = receive

    def carry(h):
        arrivals.pop(("f", h))
        arrive("x", h)
        res = acc[1, h] - x_in[h].astype(F32)

        def term(owner):
            at = pl.ds(pl.multiple_of(owner * local_rows, local_rows), local_rows)
            return dot(f_all[h, owner], lnk_v[:, at], NT)

        for other, steps in ((0, (0, 1, 3, 2)), (1, (0, 1)), (1, (3, 2))):
            owners = [lax.rem(x_lo + other, 2) * 4 + lax.rem(y + step, 4) for step in steps]
            for owner, step in zip(owners, steps):
                if other or step:
                    f_wait(h, owner)
            res = res - sum(term(owner) for owner in owners)
        solve_send(1, h, res.astype(BF16), c_out, c_in, c_sem)

    def finish(h):
        second = solve_receive(1, h, c_in)
        both = jnp.stack([f_all[h, row].astype(F32), second.astype(F32)], axis=1)
        out[pl.ds(h * part_rows, part_rows)] = both.astype(BF16)

    def a_step(h):
        if h == 0:
            arrive("inverse", 0)
        solve_send(0, h, first_residual(h), a_out, a_in, a_sem)

    def carry_step(h):
        if h == 0:
            arrive("link")
            arrive("inverse", 1)
        carry(h)

    program = (
        lambda: sibling_part(0, 0), lambda: own_part(0, 0),
        lambda: sibling_part(0, 1), lambda: add_sibling(0, 0), lambda: own_part(0, 1),
        lambda: sibling_part(1, 0), lambda: add_sibling(0, 1), lambda: own_part(1, 0),
        lambda: sibling_part(1, 1), lambda: add_sibling(1, 0),
        lambda: own_part(1, 1),
        lambda: a_step(0),
        lambda: z_send(0), lambda: add_sibling(1, 1),
        lambda: a_step(1),
        lambda: z_send(1),
        lambda: first_send(0),
        lambda: second_sum_over_z(0),
        lambda: first_send(1),
        lambda: second_sum_over_z(1),
        lambda: carry_step(0), lambda: carry_step(1),
        lambda: finish(0), lambda: finish(1),
    )
    for step in program[:stages]:
        step()
    for wait in [*arrivals.values(), *drains]:
        wait()


def local(rhs, solved, panel, inverse, link, stages=None):
    samples, _, local_rows = rhs.shape
    part_rows = samples // HALVES
    piece = (part_rows, local_rows)
    column = (HALVES, SLOTS * part_rows, local_rows)
    any_spec = pl.BlockSpec(memory_space=pl.ANY)
    dma = pltpu.SemaphoreType.DMA
    return pl.pallas_call(
        functools.partial(kernel, stages),
        out_shape=pltpu.VMEM(rhs.shape, BF16),
        in_specs=[any_spec] * 5,
        out_specs=pl.BlockSpec(memory_space=pltpu.VMEM),
        scratch_shapes=[
            pltpu.VMEM((2, HALVES, SLOTS * part_rows, solved.shape[1]), BF16),
            pltpu.VMEM(panel.shape, BF16),
            pltpu.VMEM(inverse.shape, BF16),
            pltpu.VMEM(link.shape, BF16),
            pltpu.VMEM(rhs.shape, BF16),
            pltpu.VMEM((2,) + column, BF16),
            pltpu.VMEM((2,) + column, BF16),
            pltpu.VMEM((SLOTS * part_rows, local_rows), F32),
            pltpu.VMEM((2,) + column, BF16),
            pltpu.VMEM((2,) + column, BF16),
            pltpu.VMEM((HALVES,) + piece, BF16),
            pltpu.VMEM((HALVES,) + piece, BF16),
            pltpu.VMEM((HALVES,) + piece, F32),
            pltpu.VMEM((2, HALVES) + piece, F32),
            pltpu.VMEM((2, HALVES, ROWS) + piece, F32),
            pltpu.VMEM((HALVES, ROWS) + piece, BF16),
            pltpu.VMEM((HALVES, ROWS) + piece, BF16),
            pltpu.VMEM((HALVES, ROWS) + piece, BF16),
            pltpu.VMEM((HALVES, ROWS) + piece, BF16),
            pltpu.VMEM((HALVES, ROWS) + piece, BF16),
            dma((38,)),
            dma((2, 2, HALVES)),
            dma((2, 2, HALVES, SLOTS)),
            dma((2, HALVES)),
            dma((2, HALVES, ROWS)),
            dma((2, HALVES, ROWS)),
            dma((2, HALVES, ROWS)),
        ],
        compiler_params=pltpu.CompilerParams(
            collective_id=0 if stages is None else stages, has_side_effects=True, vmem_limit_bytes=56 << 20
        ),
        cost_estimate=pl.CostEstimate(
            flops=4 * solved.shape[0] * solved.shape[1] * local_rows, bytes_accessed=24 << 20, transcendentals=0
        ),
        name="window_solve" if stages is None else f"stage{stages:02d}",
    )(solved, panel, inverse, link, rhs)


def solution(mesh):
    return jax.shard_map(
        local,
        mesh=mesh,
        in_specs=(
            P("col", None, "row"),
            P(None, "col"),
            P(None, "row", "col"),
            P(None, "row", None),
            P("row", None),
        ),
        out_specs=P("col", None, "row"),
        check_vma=False,
    )
```

```python
import functools

import jax
import jax.numpy as jnp
from jax import lax
from jax.experimental import pallas as pl
from jax.experimental.pallas import tpu as pltpu
from jax.sharding import PartitionSpec as P

MESH = pl.DeviceIdType.MESH
BF16 = jnp.bfloat16
F32 = jnp.float32
NT = (((1,), (1,)), ((), ()))
NN = (((1,), (0,)), ((), ()))
ROWS = 8
F_ORDER = ((1, 2), (1, 1), (1, 3), (0, 2), (1, 0), (0, 1), (0, 3))
SLOTS = 8
Y_OFFSETS = Z_OFFSETS = (2, 1, 3, 0)
HALVES = 2


def dot(left, right, dims):
    return lax.dot_general(left, right, dims, preferred_element_type=F32)


def kernel(
    stages, solved, panel, inverse, link, rhs, out,
    sol_v, pan_v, inv_v, lnk_v, rhs_v,
    core_out, core_in, own, col_out, col_in, x_out, x_in, keep, acc,
    part, a_out, a_in, f_all, c_out, c_in,
    load_sem, core_sem, col_sem, x_sem, a_sem, f_sem, c_sem,
):
    samples, local_rows = rhs.shape[0], rhs.shape[2]
    part_rows = samples // HALVES
    row, col = lax.axis_index("row"), lax.axis_index("col")
    x_lo, y = row // 4, row % 4
    x_hi, z, core = col // 8, (col // 2) % 4, col % 2
    drains, arrivals = [], {}

    def col_of(dx, dz, k):
        return lax.rem(x_hi + dx, 2) * 8 + lax.rem(z + dz, 4) * 2 + k

    def remote(src, dst, send_sem, recv_sem, device):
        return pltpu.make_async_remote_copy(
            src_ref=src, dst_ref=dst, send_sem=send_sem, recv_sem=recv_sem,
            device_id=device, device_id_type=MESH,
        )

    def start(copy, *key):
        copy.start()
        drains.append(copy.wait_send)
        arrivals[key] = copy.wait_recv

    def arrive(*key):
        arrivals.pop(key)()

    def slot_of(s):
        return Z_OFFSETS[s // 2], 1 - s % 2

    def slot_rows(s, count=1):
        return pl.ds(s * part_rows, count * part_rows)

    def load_sol(kind, h, s):
        dz, dx = slot_of(s)
        c = col_of(dx, dz, 1 - core if kind == 0 else core)
        at = pl.multiple_of(c * samples + h * part_rows, part_rows)
        return pltpu.make_async_copy(
            solved.at[pl.ds(at, part_rows)], sol_v.at[kind, h, slot_rows(s)],
            load_sem.at[(kind * HALVES + h) * SLOTS + s],
        )

    load_panel = [pltpu.make_async_copy(panel.at[b], pan_v.at[b], load_sem.at[32 + b]) for b in range(2)]
    load_inv = [pltpu.make_async_copy(inverse.at[b], inv_v.at[b], load_sem.at[34 + b]) for b in range(2)]
    load_link = pltpu.make_async_copy(link, lnk_v, load_sem.at[36])
    load_rhs = pltpu.make_async_copy(rhs, rhs_v, load_sem.at[37])
    def load(copy, *key):
        copy.start()
        arrivals[key] = copy.wait

    def load_half(kind, h):
        for s in range(SLOTS):
            load(load_sol(kind, h, s), "sol", kind, h, s)

    load(load_panel[0], "panel", 0)
    load_half(0, 0)
    load_half(1, 0)
    load(load_rhs, "rhs")
    load_half(0, 1)
    load_half(1, 1)

    barrier = pltpu.get_barrier_semaphore()
    for i in range(1, ROWS):
        pl.semaphore_signal(barrier, inc=1, device_id=(lax.rem(row + i, ROWS), col), device_id_type=MESH)
    for s in range(SLOTS - 1):
        dz, dx = slot_of(s)
        pl.semaphore_signal(barrier, inc=1, device_id=(row, col_of(dx, dz, core)), device_id_type=MESH)
    sibling = (row, col_of(0, 0, 1 - core))
    pl.semaphore_signal(barrier, inc=1, device_id=sibling, device_id_type=MESH)

    def take_rhs():
        arrive("rhs")
        rhs_all = rhs_v[...].astype(F32)
        for b in range(2):
            for h in range(HALVES):
                acc[b, h] = rhs_all[h * part_rows : (h + 1) * part_rows, b, :]

    def core_copy(b, h):
        return remote(core_out.at[b, h], core_in.at[b, h], core_sem.at[0, b, h], core_sem.at[1, b, h], sibling)

    def col_copy(h, s):
        dz, dx = slot_of(s)
        return remote(
            col_out.at[0, h, slot_rows(s)], col_in.at[0, h, slot_rows(s)],
            col_sem.at[0, 0, h, s], col_sem.at[1, 0, h, s], (row, col_of(dx, dz, core)),
        )

    def z_copy(h, i):
        at = slot_rows(2 * i, 2)
        return remote(
            col_out.at[1, h, at], col_in.at[1, h, at],
            col_sem.at[0, 1, h, i], col_sem.at[1, 1, h, i], (row, col_of(0, Z_OFFSETS[i], core)),
        )

    def x_copy(h):
        return remote(x_out.at[h], x_in.at[h], x_sem.at[0, h], x_sem.at[1, h], (row, col_of(1, 0, core)))

    def sibling_part(b, h):
        if b == 0:
            for s in range(SLOTS):
                arrive("sol", 0, h, s)
        if h == 0:
            arrive("panel", b)
        if (b, h) == (0, 1):
            load(load_panel[1], "panel", 1)
            load(load_inv[0], "inverse", 0)
        core_out[b, h] = dot(sol_v[0, h], pan_v[b], NT).astype(BF16)
        if (b, h) == (0, 0):
            pl.semaphore_wait(barrier, 15)
        start(core_copy(b, h), "core", b, h)

    def own_part(b, h):
        if b == 0:
            for s in range(SLOTS):
                arrive("sol", 1, h, s)
        if (b, h) == (0, 1):
            load(load_link, "link")
            load(load_inv[1], "inverse", 1)
        own[...] = dot(sol_v[1, h], pan_v[b], NT)

    def add_sibling(b, h):
        arrive("core", b, h)
        last = 7 * part_rows
        if b == 0:
            col_out[0, h, slot_rows(0, 7)] = (own[:last] + core_in[0, h, :last].astype(F32)).astype(BF16)
            for s in range(SLOTS - 1):
                start(col_copy(h, s), "col", h, s)
        else:
            sent = 6 * part_rows
            col_out[1, h, slot_rows(0, 6)] = (own[:sent] + core_in[1, h, :sent].astype(F32)).astype(BF16)
            keep[h] = own[sent:last] + core_in[1, h, sent:last].astype(F32)
        if (b, h) == (0, 0):
            clear()
            take_rhs()
        acc[b, h] -= own[last:] + core_in[b, h, last:].astype(F32)

    def z_send(h):
        for i in range(3):
            start(z_copy(h, i), "z", h, i)

    def first_residual(h):
        for s in range(SLOTS - 1):
            arrive("col", h, s)
        res = acc[0, h]
        for s in range(SLOTS - 1):
            res = res - col_in[0, h, slot_rows(s)].astype(F32)
        return res.astype(BF16)

    def second_sum_over_z(h):
        for i in range(3):
            arrive("z", h, i)
        there, here = keep[h], acc[1, h]
        for i in range(3):
            there = there + col_in[1, h, slot_rows(2 * i)].astype(F32)
            here = here - col_in[1, h, slot_rows(2 * i + 1)].astype(F32)
        x_out[h] = there.astype(BF16)
        start(x_copy(h), "x", h)
        acc[1, h] = here

    def solve_copy(outgoing, incoming, sems, h, j):
        return remote(outgoing.at[h, j], incoming.at[h, row], sems.at[0, h, j], sems.at[1, h, row], (j, col))

    def solve_send(b, h, res, outgoing, incoming, sems):
        def group(base):
            for j in range(4 * base, 4 * base + 4):
                product = dot(res, inv_v[b, :, j * local_rows : (j + 1) * local_rows], NN)
                part[b, h, j] = product
                outgoing[h, j] = product.astype(BF16)
            for dy in Y_OFFSETS:
                j = 4 * base + lax.rem(y + dy, 4)

                @pl.when(row < j)
                def _():
                    solve_copy(outgoing, incoming, sems, h, j).start()

        group(1)

        @pl.when(row < 4)
        def _():
            group(0)

        def drain():
            for j in range(1, ROWS):
                @pl.when(row < j)
                def _():
                    solve_copy(outgoing, incoming, sems, h, j).wait_send()

        def wait(i):
            pltpu.make_async_remote_copy(
                src_ref=incoming.at[h, i], dst_ref=incoming.at[h, i],
                send_sem=sems.at[0, h, i], recv_sem=sems.at[1, h, i],
                device_id=(row, col), device_id_type=MESH,
            ).wait_recv()

        def receive():
            for i in range(ROWS - 1):
                pl.when(row > i)(functools.partial(wait, i))

        drains.append(drain)
        arrivals["solve", b, h] = receive

    def solve_receive(b, h, incoming):
        arrive("solve", b, h)
        total = part[b, h, row]
        for i in range(ROWS - 1):
            total = total + incoming[h, i].astype(F32)
        return total.astype(BF16)

    def clear():
        for i in range(ROWS - 1):
            @pl.when(row <= i)
            def _():
                a_in[:, i] = jnp.zeros_like(a_in[:, i])
                c_in[:, i] = jnp.zeros_like(c_in[:, i])

    def f_copy(h, i):
        dx, dy = F_ORDER[i]
        return remote(
            f_all.at[h, row], f_all.at[h, row], f_sem.at[0, h, i], f_sem.at[1, h, row],
            (lax.rem(x_lo + dx, 2) * 4 + lax.rem(y + dy, 4), col),
        )

    def f_wait(h, owner):
        remote(
            f_all.at[h, owner], f_all.at[h, owner], f_sem.at[0, h, owner], f_sem.at[1, h, owner], (row, col)
        ).wait_recv()

    def first_send(h):
        f_all[h, row] = solve_receive(0, h, a_in)
        for i in range(ROWS - 1):
            copy = f_copy(h, i)
            copy.start()
            drains.append(copy.wait_send)

        def receive():
            for owner in range(ROWS):
                pl.when(row != owner)(functools.partial(f_wait, h, owner))

        arrivals["f", h] = receive

    def carry(h):
        arrivals.pop(("f", h))
        res = acc[1, h]

        def term(owner):
            at = pl.ds(pl.multiple_of(owner * local_rows, local_rows), local_rows)
            return dot(f_all[h, owner], lnk_v[:, at], NT)

        for other, steps in ((0, (0, 1, 3, 2)), (1, (0, 1)), (1, (3, 2))):
            owners = [lax.rem(x_lo + other, 2) * 4 + lax.rem(y + step, 4) for step in steps]
            for owner, step in zip(owners, steps):
                if other or step:
                    f_wait(h, owner)
            res = res - sum(term(owner) for owner in owners)
        arrive("x", h)
        res = res - x_in[h].astype(F32)
        solve_send(1, h, res.astype(BF16), c_out, c_in, c_sem)

    def finish(h):
        second = solve_receive(1, h, c_in)
        both = jnp.stack([f_all[h, row].astype(F32), second.astype(F32)], axis=1)
        out[pl.ds(h * part_rows, part_rows)] = both.astype(BF16)

    def a_step(h):
        if h == 0:
            arrive("inverse", 0)
        solve_send(0, h, first_residual(h), a_out, a_in, a_sem)

    def carry_step(h):
        if h == 0:
            arrive("link")
            arrive("inverse", 1)
        carry(h)

    program = (
        lambda: sibling_part(0, 0), lambda: own_part(0, 0),
        lambda: sibling_part(0, 1), lambda: add_sibling(0, 0), lambda: own_part(0, 1),
        lambda: sibling_part(1, 0), lambda: add_sibling(0, 1), lambda: own_part(1, 0),
        lambda: sibling_part(1, 1), lambda: add_sibling(1, 0),
        lambda: z_send(0), lambda: own_part(1, 1),
        lambda: a_step(0),
        lambda: add_sibling(1, 1), lambda: z_send(1),
        lambda: a_step(1),
        lambda: second_sum_over_z(0),
        lambda: first_send(0),
        lambda: second_sum_over_z(1),
        lambda: first_send(1),
        lambda: carry_step(0), lambda: carry_step(1),
        lambda: finish(0), lambda: finish(1),
    )
    for step in program[:stages]:
        step()
    for wait in [*arrivals.values(), *drains]:
        wait()


def local(rhs, solved, panel, inverse, link, stages=None):
    samples, _, local_rows = rhs.shape
    part_rows = samples // HALVES
    piece = (part_rows, local_rows)
    column = (HALVES, SLOTS * part_rows, local_rows)
    any_spec = pl.BlockSpec(memory_space=pl.ANY)
    dma = pltpu.SemaphoreType.DMA
    return pl.pallas_call(
        functools.partial(kernel, stages),
        out_shape=pltpu.VMEM(rhs.shape, BF16),
        in_specs=[any_spec] * 5,
        out_specs=pl.BlockSpec(memory_space=pltpu.VMEM),
        scratch_shapes=[
            pltpu.VMEM((2, HALVES, SLOTS * part_rows, solved.shape[1]), BF16),
            pltpu.VMEM(panel.shape, BF16),
            pltpu.VMEM(inverse.shape, BF16),
            pltpu.VMEM(link.shape, BF16),
            pltpu.VMEM(rhs.shape, BF16),
            pltpu.VMEM((2,) + column, BF16),
            pltpu.VMEM((2,) + column, BF16),
            pltpu.VMEM((SLOTS * part_rows, local_rows), F32),
            pltpu.VMEM((2,) + column, BF16),
            pltpu.VMEM((2,) + column, BF16),
            pltpu.VMEM((HALVES,) + piece, BF16),
            pltpu.VMEM((HALVES,) + piece, BF16),
            pltpu.VMEM((HALVES,) + piece, F32),
            pltpu.VMEM((2, HALVES) + piece, F32),
            pltpu.VMEM((2, HALVES, ROWS) + piece, F32),
            pltpu.VMEM((HALVES, ROWS) + piece, BF16),
            pltpu.VMEM((HALVES, ROWS) + piece, BF16),
            pltpu.VMEM((HALVES, ROWS) + piece, BF16),
            pltpu.VMEM((HALVES, ROWS) + piece, BF16),
            pltpu.VMEM((HALVES, ROWS) + piece, BF16),
            dma((38,)),
            dma((2, 2, HALVES)),
            dma((2, 2, HALVES, SLOTS)),
            dma((2, HALVES)),
            dma((2, HALVES, ROWS)),
            dma((2, HALVES, ROWS)),
            dma((2, HALVES, ROWS)),
        ],
        compiler_params=pltpu.CompilerParams(
            collective_id=0 if stages is None else stages, has_side_effects=True, vmem_limit_bytes=56 << 20
        ),
        cost_estimate=pl.CostEstimate(
            flops=4 * solved.shape[0] * solved.shape[1] * local_rows, bytes_accessed=24 << 20, transcendentals=0
        ),
        name="window_solve" if stages is None else f"stage{stages:02d}",
    )(solved, panel, inverse, link, rhs)


def solution(mesh):
    return jax.shard_map(
        local,
        mesh=mesh,
        in_specs=(
            P("col", None, "row"),
            P(None, "col"),
            P(None, "row", "col"),
            P(None, "row", None),
            P("row", None),
        ),
        out_specs=P("col", None, "row"),
        check_vma=False,
    )
```

```python
import functools

import jax
import jax.numpy as jnp
from jax import lax
from jax.experimental import pallas as pl
from jax.experimental.pallas import tpu as pltpu
from jax.sharding import PartitionSpec as P

MESH = pl.DeviceIdType.MESH
BF16 = jnp.bfloat16
F32 = jnp.float32
NT = (((1,), (1,)), ((), ()))
NN = (((1,), (0,)), ((), ()))
ROWS = 8
F_ORDER = ((1, 2), (0, 2), (1, 1), (1, 3), (0, 1), (0, 3), (1, 0))
SLOTS = 8
Y_OFFSETS = Z_OFFSETS = (2, 1, 3, 0)
HALVES = 2


def dot(left, right, dims):
    return lax.dot_general(left, right, dims, preferred_element_type=F32)


def kernel(
    stages, solved, panel, inverse, link, rhs, out,
    sol_v, pan_v, inv_v, lnk_v, rhs_v,
    core_out, core_in, own, col_out, col_in, x_out, x_in, keep, acc,
    part, a_out, a_in, f_all, c_out, c_in,
    load_sem, core_sem, col_sem, x_sem, a_sem, f_sem, c_sem,
):
    samples, local_rows = rhs.shape[0], rhs.shape[2]
    part_rows = samples // HALVES
    row, col = lax.axis_index("row"), lax.axis_index("col")
    x_lo, y = row // 4, row % 4
    x_hi, z, core = col // 8, (col // 2) % 4, col % 2
    drains, arrivals = [], {}

    def col_of(dx, dz, k):
        return lax.rem(x_hi + dx, 2) * 8 + lax.rem(z + dz, 4) * 2 + k

    def remote(src, dst, send_sem, recv_sem, device):
        return pltpu.make_async_remote_copy(
            src_ref=src, dst_ref=dst, send_sem=send_sem, recv_sem=recv_sem,
            device_id=device, device_id_type=MESH,
        )

    def start(copy, *key):
        copy.start()
        drains.append(copy.wait_send)
        arrivals[key] = copy.wait_recv

    def arrive(*key):
        arrivals.pop(key)()

    def slot_of(s):
        return Z_OFFSETS[s // 2], 1 - s % 2

    def slot_rows(s, count=1):
        return pl.ds(s * part_rows, count * part_rows)

    def load_sol(kind, h, s):
        dz, dx = slot_of(s)
        c = col_of(dx, dz, 1 - core if kind == 0 else core)
        at = pl.multiple_of(c * samples + h * part_rows, part_rows)
        return pltpu.make_async_copy(
            solved.at[pl.ds(at, part_rows)], sol_v.at[kind, h, slot_rows(s)],
            load_sem.at[(kind * HALVES + h) * SLOTS + s],
        )

    load_panel = [pltpu.make_async_copy(panel.at[b], pan_v.at[b], load_sem.at[32 + b]) for b in range(2)]
    load_inv = [pltpu.make_async_copy(inverse.at[b], inv_v.at[b], load_sem.at[34 + b]) for b in range(2)]
    load_link = pltpu.make_async_copy(link, lnk_v, load_sem.at[36])
    load_rhs = pltpu.make_async_copy(rhs, rhs_v, load_sem.at[37])
    def load(copy, *key):
        copy.start()
        arrivals[key] = copy.wait

    def load_half(kind, h):
        for s in range(SLOTS):
            load(load_sol(kind, h, s), "sol", kind, h, s)

    load(load_panel[0], "panel", 0)
    load_half(0, 0)
    load_half(1, 0)
    load(load_rhs, "rhs")
    load_half(0, 1)
    load_half(1, 1)

    barrier = pltpu.get_barrier_semaphore()
    for i in range(1, ROWS):
        pl.semaphore_signal(barrier, inc=1, device_id=(lax.rem(row + i, ROWS), col), device_id_type=MESH)
    for s in range(SLOTS - 1):
        dz, dx = slot_of(s)
        pl.semaphore_signal(barrier, inc=1, device_id=(row, col_of(dx, dz, core)), device_id_type=MESH)
    sibling = (row, col_of(0, 0, 1 - core))
    pl.semaphore_signal(barrier, inc=1, device_id=sibling, device_id_type=MESH)

    def take_rhs():
        arrive("rhs")
        rhs_all = rhs_v[...].astype(F32)
        for b in range(2):
            for h in range(HALVES):
                acc[b, h] = rhs_all[h * part_rows : (h + 1) * part_rows, b, :]

    def core_copy(b, h):
        return remote(core_out.at[b, h], core_in.at[b, h], core_sem.at[0, b, h], core_sem.at[1, b, h], sibling)

    def col_copy(h, s):
        dz, dx = slot_of(s)
        return remote(
            col_out.at[0, h, slot_rows(s)], col_in.at[0, h, slot_rows(s)],
            col_sem.at[0, 0, h, s], col_sem.at[1, 0, h, s], (row, col_of(dx, dz, core)),
        )

    def z_copy(h, i):
        at = slot_rows(2 * i, 2)
        return remote(
            col_out.at[1, h, at], col_in.at[1, h, at],
            col_sem.at[0, 1, h, i], col_sem.at[1, 1, h, i], (row, col_of(0, Z_OFFSETS[i], core)),
        )

    def x_copy(h):
        return remote(x_out.at[h], x_in.at[h], x_sem.at[0, h], x_sem.at[1, h], (row, col_of(1, 0, core)))

    def sibling_part(b, h):
        if b == 0:
            for s in range(SLOTS):
                arrive("sol", 0, h, s)
        if h == 0:
            arrive("panel", b)
        if (b, h) == (0, 1):
            load(load_panel[1], "panel", 1)
            load(load_inv[0], "inverse", 0)
        core_out[b, h] = dot(sol_v[0, h], pan_v[b], NT).astype(BF16)
        if (b, h) == (0, 0):
            pl.semaphore_wait(barrier, 15)
        start(core_copy(b, h), "core", b, h)

    def own_part(b, h):
        if b == 0:
            for s in range(SLOTS):
                arrive("sol", 1, h, s)
        if (b, h) == (0, 1):
            load(load_link, "link")
            load(load_inv[1], "inverse", 1)
        own[...] = dot(sol_v[1, h], pan_v[b], NT)

    def add_sibling(b, h):
        arrive("core", b, h)
        last = 7 * part_rows
        if b == 0:
            col_out[0, h, slot_rows(0, 7)] = (own[:last] + core_in[0, h, :last].astype(F32)).astype(BF16)
            for s in range(SLOTS - 1):
                start(col_copy(h, s), "col", h, s)
        else:
            sent = 6 * part_rows
            col_out[1, h, slot_rows(0, 6)] = (own[:sent] + core_in[1, h, :sent].astype(F32)).astype(BF16)
            keep[h] = own[sent:last] + core_in[1, h, sent:last].astype(F32)
        if (b, h) == (0, 0):
            clear()
            take_rhs()
        acc[b, h] -= own[last:] + core_in[b, h, last:].astype(F32)

    def z_send(h):
        for i in range(3):
            start(z_copy(h, i), "z", h, i)

    def first_residual(h):
        for s in range(SLOTS - 1):
            arrive("col", h, s)
        res = acc[0, h]
        for s in range(SLOTS - 1):
            res = res - col_in[0, h, slot_rows(s)].astype(F32)
        return res.astype(BF16)

    def second_sum_over_z(h):
        for i in range(3):
            arrive("z", h, i)
        there, here = keep[h], acc[1, h]
        for i in range(3):
            there = there + col_in[1, h, slot_rows(2 * i)].astype(F32)
            here = here - col_in[1, h, slot_rows(2 * i + 1)].astype(F32)
        x_out[h] = there.astype(BF16)
        start(x_copy(h), "x", h)
        acc[1, h] = here

    def solve_copy(outgoing, incoming, sems, h, j):
        return remote(outgoing.at[h, j], incoming.at[h, row], sems.at[0, h, j], sems.at[1, h, row], (j, col))

    def solve_send(b, h, res, outgoing, incoming, sems):
        def group(base):
            for j in range(4 * base, 4 * base + 4):
                product = dot(res, inv_v[b, :, j * local_rows : (j + 1) * local_rows], NN)
                part[b, h, j] = product
                outgoing[h, j] = product.astype(BF16)
            for dy in Y_OFFSETS:
                j = 4 * base + lax.rem(y + dy, 4)

                @pl.when(row < j)
                def _():
                    solve_copy(outgoing, incoming, sems, h, j).start()

        group(1)

        @pl.when(row < 4)
        def _():
            group(0)

        def drain():
            for j in range(1, ROWS):
                @pl.when(row < j)
                def _():
                    solve_copy(outgoing, incoming, sems, h, j).wait_send()

        def wait(i):
            pltpu.make_async_remote_copy(
                src_ref=incoming.at[h, i], dst_ref=incoming.at[h, i],
                send_sem=sems.at[0, h, i], recv_sem=sems.at[1, h, i],
                device_id=(row, col), device_id_type=MESH,
            ).wait_recv()

        def receive():
            for i in range(ROWS - 1):
                pl.when(row > i)(functools.partial(wait, i))

        drains.append(drain)
        arrivals["solve", b, h] = receive

    def solve_receive(b, h, incoming):
        arrive("solve", b, h)
        total = part[b, h, row]
        for i in range(ROWS - 1):
            total = total + incoming[h, i].astype(F32)
        return total.astype(BF16)

    def clear():
        for i in range(ROWS - 1):
            @pl.when(row <= i)
            def _():
                a_in[:, i] = jnp.zeros_like(a_in[:, i])
                c_in[:, i] = jnp.zeros_like(c_in[:, i])

    def f_copy(h, i):
        dx, dy = F_ORDER[i]
        return remote(
            f_all.at[h, row], f_all.at[h, row], f_sem.at[0, h, i], f_sem.at[1, h, row],
            (lax.rem(x_lo + dx, 2) * 4 + lax.rem(y + dy, 4), col),
        )

    def f_wait(h, owner):
        remote(
            f_all.at[h, owner], f_all.at[h, owner], f_sem.at[0, h, owner], f_sem.at[1, h, owner], (row, col)
        ).wait_recv()

    def first_send(h):
        f_all[h, row] = solve_receive(0, h, a_in)
        for i in range(ROWS - 1):
            copy = f_copy(h, i)
            copy.start()
            drains.append(copy.wait_send)

        def receive():
            for owner in range(ROWS):
                pl.when(row != owner)(functools.partial(f_wait, h, owner))

        arrivals["f", h] = receive

    def carry(h):
        arrivals.pop(("f", h))
        res = acc[1, h]

        def term(owner):
            at = pl.ds(pl.multiple_of(owner * local_rows, local_rows), local_rows)
            return dot(f_all[h, owner], lnk_v[:, at], NT)

        for other, steps in ((0, (0, 1, 3, 2)), (1, (0, 1)), (1, (3, 2))):
            owners = [lax.rem(x_lo + other, 2) * 4 + lax.rem(y + step, 4) for step in steps]
            for owner, step in zip(owners, steps):
                if other or step:
                    f_wait(h, owner)
            res = res - sum(term(owner) for owner in owners)
        arrive("x", h)
        res = res - x_in[h].astype(F32)
        solve_send(1, h, res.astype(BF16), c_out, c_in, c_sem)

    def finish(h):
        second = solve_receive(1, h, c_in)
        both = jnp.stack([f_all[h, row].astype(F32), second.astype(F32)], axis=1)
        out[pl.ds(h * part_rows, part_rows)] = both.astype(BF16)

    def a_step(h):
        if h == 0:
            arrive("inverse", 0)
        solve_send(0, h, first_residual(h), a_out, a_in, a_sem)

    def carry_step(h):
        if h == 0:
            arrive("link")
            arrive("inverse", 1)
        carry(h)

    program = (
        lambda: sibling_part(0, 0), lambda: own_part(0, 0),
        lambda: sibling_part(0, 1), lambda: add_sibling(0, 0), lambda: own_part(0, 1),
        lambda: sibling_part(1, 0), lambda: add_sibling(0, 1), lambda: own_part(1, 0),
        lambda: sibling_part(1, 1), lambda: add_sibling(1, 0),
        lambda: z_send(0), lambda: own_part(1, 1),
        lambda: a_step(0),
        lambda: add_sibling(1, 1), lambda: z_send(1),
        lambda: a_step(1),
        lambda: second_sum_over_z(0),
        lambda: first_send(0),
        lambda: second_sum_over_z(1),
        lambda: first_send(1),
        lambda: carry_step(0), lambda: carry_step(1),
        lambda: finish(0), lambda: finish(1),
    )
    for step in program[:stages]:
        step()
    for wait in [*arrivals.values(), *drains]:
        wait()


def local(rhs, solved, panel, inverse, link, stages=None):
    samples, _, local_rows = rhs.shape
    part_rows = samples // HALVES
    piece = (part_rows, local_rows)
    column = (HALVES, SLOTS * part_rows, local_rows)
    any_spec = pl.BlockSpec(memory_space=pl.ANY)
    dma = pltpu.SemaphoreType.DMA
    return pl.pallas_call(
        functools.partial(kernel, stages),
        out_shape=pltpu.VMEM(rhs.shape, BF16),
        in_specs=[any_spec] * 5,
        out_specs=pl.BlockSpec(memory_space=pltpu.VMEM),
        scratch_shapes=[
            pltpu.VMEM((2, HALVES, SLOTS * part_rows, solved.shape[1]), BF16),
            pltpu.VMEM(panel.shape, BF16),
            pltpu.VMEM(inverse.shape, BF16),
            pltpu.VMEM(link.shape, BF16),
            pltpu.VMEM(rhs.shape, BF16),
            pltpu.VMEM((2,) + column, BF16),
            pltpu.VMEM((2,) + column, BF16),
            pltpu.VMEM((SLOTS * part_rows, local_rows), F32),
            pltpu.VMEM((2,) + column, BF16),
            pltpu.VMEM((2,) + column, BF16),
            pltpu.VMEM((HALVES,) + piece, BF16),
            pltpu.VMEM((HALVES,) + piece, BF16),
            pltpu.VMEM((HALVES,) + piece, F32),
            pltpu.VMEM((2, HALVES) + piece, F32),
            pltpu.VMEM((2, HALVES, ROWS) + piece, F32),
            pltpu.VMEM((HALVES, ROWS) + piece, BF16),
            pltpu.VMEM((HALVES, ROWS) + piece, BF16),
            pltpu.VMEM((HALVES, ROWS) + piece, BF16),
            pltpu.VMEM((HALVES, ROWS) + piece, BF16),
            pltpu.VMEM((HALVES, ROWS) + piece, BF16),
            dma((38,)),
            dma((2, 2, HALVES)),
            dma((2, 2, HALVES, SLOTS)),
            dma((2, HALVES)),
            dma((2, HALVES, ROWS)),
            dma((2, HALVES, ROWS)),
            dma((2, HALVES, ROWS)),
        ],
        compiler_params=pltpu.CompilerParams(
            collective_id=0 if stages is None else stages, has_side_effects=True, vmem_limit_bytes=56 << 20
        ),
        cost_estimate=pl.CostEstimate(
            flops=4 * solved.shape[0] * solved.shape[1] * local_rows, bytes_accessed=24 << 20, transcendentals=0
        ),
        name="window_solve" if stages is None else f"stage{stages:02d}",
    )(solved, panel, inverse, link, rhs)


def solution(mesh):
    return jax.shard_map(
        local,
        mesh=mesh,
        in_specs=(
            P("col", None, "row"),
            P(None, "col"),
            P(None, "row", "col"),
            P(None, "row", None),
            P("row", None),
        ),
        out_specs=P("col", None, "row"),
        check_vma=False,
    )
```
